512 devices in a mesh: pipe: 8 (over z_lo), dp: 16 (over x, z_hi, core), tensor: 4 (over y).
Axes of the slice: x: 4, y: 4, z: 16 (z_hi: 2, z_lo: 8; z = z_hi * 8 + z_lo), core: 2. Of those that a mesh axis runs over, the one named last changes fastest.
Arguments:
- outputs: bfloat16 [8, 2048, 6144], P('pipe', 'dp', 'tensor'), may hold values from -6 to 6
- cotangents: bfloat16 [4, 8, 2048, 6144], P(None, 'pipe', 'dp', 'tensor'), may hold values from -3 to 3
- gains: bfloat16 [8, 6144], P('pipe', 'tensor'), may hold values from 0.099609375 to 1.8984375
- first_weight: bfloat16 [8, 6144, 256], P('pipe', 'tensor'), may hold values from -0.078125 to 0.078125
- second_weight: bfloat16 [8, 256, 32], P('pipe'), may hold values from -0.375 to 0.375
Outputs:
- output_grads: bfloat16 [8, 2048, 6144], P('pipe', 'dp', 'tensor')
- first_grads: float32 [8, 6144, 256], P('pipe', 'tensor')
- second_grads: float32 [8, 256, 32], P('pipe')
The draws below stay inside these ranges and needn't reach their ends.
All inputs are finite; a program needn't handle non-finite values.
Results may differ from the reference program's by a relative error of at most 0.025.
Values may be sent and summed in bfloat16 or wider, within the bound.
No kernel may reach another device: no remote copies, remote signals or barrier semaphores. Data moves between devices by JAX's collectives and lax.ppermute only.
A program may use at most 64 MiB of HBM per device.

```python
import jax
import jax.numpy as jnp
from jax import lax

D = 6144
GEN = 256
LAYERS = 8
TOKENS = 2048


def block_levels(key, extent, cuts, least, high):
    gain = 1.0
    for axis_at, blocks in cuts:
        heights = jax.random.uniform(jax.random.fold_in(jax.random.fold_in(key, 6), axis_at), (blocks,), jnp.float32, least / len(cuts), high / len(cuts))
        gain = gain * jnp.repeat(jnp.exp(heights), extent[axis_at] // blocks).reshape((-1,) + (1,) * (len(extent) - 1 - axis_at))
    return gain


def bell_draw(stream_key, extent, deviation, bound, shards=(), kind=jnp.bfloat16):
    entries = jax.random.normal(stream_key, extent, jnp.float32) * deviation
    if len(shards) > 0:
        entries = block_levels(stream_key, extent, shards, -0.22, 0.18) * entries
    return jnp.clip(entries, min=-bound, max=bound).astype(kind)


def setup_inputs(seed: int = 0) -> dict:
    arg_keys = jax.random.split(jax.random.key(seed), 6)
    outputs = bell_draw(arg_keys[0], (LAYERS, TOKENS, D), 1.0, 6.0, ((0, 8), (1, 16), (2, 4)))
    cotangents = bell_draw(arg_keys[1], (4, LAYERS, TOKENS, D), 0.5, 3.0, ((1, 8), (2, 16), (3, 4)))
    gains = jnp.clip(1.0 + 0.18 * jax.random.normal(arg_keys[2], (LAYERS, D), jnp.float32), 0.099609375, 1.8984375).astype(jnp.bfloat16)
    first_weight = bell_draw(arg_keys[3], (LAYERS, D, GEN), D ** -0.5, 0.078125, ((0, 8), (1, 4)))
    second_weight = bell_draw(arg_keys[4], (LAYERS, GEN, 4 * LAYERS), GEN ** -0.5, 0.375, ((0, 8),))
    return {"outputs": outputs, "cotangents": cotangents, "gains": gains, "first_weight": first_weight, "second_weight": second_weight}


epsilon = 1e-06

def reference(outputs, cotangents, gains, first_weight, second_weight):
    layers = outputs.shape[0]
    tokens = outputs.shape[1]
    column_ids = jnp.arange(layers)
    received = jnp.zeros(outputs.shape, jnp.float32)
    generated = []
    first_list = []
    second_list = []
    whole = outputs.astype(jnp.float32)
    for current_layer in range(layers):
        current = whole[current_layer]
        incoming = cotangents[:, current_layer].astype(jnp.float32)
        gain_row = gains[current_layer].astype(jnp.float32)
        factor = lax.rsqrt(lax.optimization_barrier(jnp.sum(current * current, axis=1)) / D + epsilon)
        normed = (current * factor[:, None] * gain_row[None, :]).astype(jnp.bfloat16)
        preact = jnp.dot(normed, first_weight[current_layer], preferred_element_type=jnp.float32)
        active = jax.nn.gelu(preact).astype(jnp.bfloat16)
        allowed = (column_ids <= current_layer).astype(jnp.float32)
        mixing = jnp.dot(active, second_weight[current_layer], preferred_element_type=jnp.float32)
        mixing = mixing.reshape(tokens, 4, layers) * allowed[None, None, :]
        terms = jnp.zeros(outputs.shape, jnp.float32)
        for stream in range(4):
            terms = terms + jnp.transpose(mixing[:, stream, :])[:, :, None] * incoming[stream][None, :, :]
        rounded = lax.optimization_barrier(terms.astype(jnp.bfloat16))
        received = received + rounded.astype(jnp.float32)
        products = jnp.einsum('std,jtd->sjt', incoming, whole)
        products = products * allowed[None, :, None]
        depth_grads = jnp.transpose(products, (2, 0, 1)).reshape(tokens, 4 * layers).astype(jnp.bfloat16)
        dactive = jnp.dot(depth_grads, second_weight[current_layer].T, preferred_element_type=jnp.float32)
        unused, pullback = jax.vjp(jax.nn.gelu, preact)
        dpreact = pullback(dactive)[0].astype(jnp.bfloat16)
        weighted = jnp.dot(dpreact, first_weight[current_layer].T, preferred_element_type=jnp.float32) * gain_row[None, :]
        inner = lax.optimization_barrier(jnp.sum(weighted * current, axis=1))
        generated.append(factor[:, None] * weighted - current * (factor ** 3 * inner / D)[:, None])
        first_list.append(jnp.dot(normed.T, dpreact, preferred_element_type=jnp.float32) / tokens)
        second_list.append(jnp.dot(active.T, depth_grads, preferred_element_type=jnp.float32) / tokens)
    output_grads = (received + jnp.stack(generated)).astype(jnp.bfloat16)
    return (output_grads, jnp.stack(first_list), jnp.stack(second_list))
```

```python
import functools

import jax
import jax.numpy as jnp
from jax import lax
from jax.experimental import pallas as pl
from jax.experimental.pallas import tpu as pltpu
from jax.sharding import PartitionSpec as P

D = 6144
epsilon = 1e-06
SPREAD = 8
LANES = 512

f32 = jnp.float32
bf16 = jnp.bfloat16


def call(kernel, shapes, flops, moved, scratch=(), smem=0, count=0):
    return pl.pallas_call(
        kernel,
        out_shape=shapes,
        in_specs=[pl.BlockSpec(memory_space=pltpu.SMEM)] * smem
        + [pl.BlockSpec(memory_space=pltpu.VMEM)] * (count - smem),
        out_specs=[pl.BlockSpec(memory_space=pltpu.VMEM)] * len(shapes),
        scratch_shapes=list(scratch),
        compiler_params=pltpu.CompilerParams(vmem_limit_bytes=20 * 1024 * 1024),
        cost_estimate=pl.CostEstimate(flops=flops, bytes_accessed=moved, transcendentals=0),
    )


def project_kernel(x_ref, gain_ref, weight_ref, packed_ref, scaled_ref):
    hidden = weight_ref.shape[1]
    tokens = x_ref.shape[0]
    x = x_ref[...].astype(f32)
    scaled = (x * gain_ref[...].astype(f32)).astype(bf16)
    scaled_ref[...] = scaled
    projected = jnp.dot(scaled, weight_ref[...], preferred_element_type=f32).astype(bf16)
    squares = jnp.broadcast_to(jnp.sum(x * x, axis=1, keepdims=True), (tokens, 128)).astype(bf16)
    for m in range(packed_ref.shape[0]):
        packed_ref[m, :, :hidden] = projected
        packed_ref[m, :, hidden:] = squares


def weights_of(mixed, layer, layers):
    lane = lax.broadcasted_iota(jnp.int32, mixed.shape, 1)
    return [
        jnp.sum(jnp.where(lane == jnp.where(layer < 0, -1, s * layers + layer), mixed, 0.0), axis=1, keepdims=True)
        for s in range(4)
    ]


def add_term(rows, lanes, weights, incoming_ref, total):
    for s in range(4):
        total = total + weights[s][rows] * incoming_ref[s, rows, lanes].astype(f32)
    return total


def put_products(held_ref, incoming_ref, products_ref, layer, layers):
    tokens = held_ref.shape[0]
    same = lax.broadcasted_iota(jnp.int32, (tokens, tokens), 0) == lax.broadcasted_iota(jnp.int32, (tokens, tokens), 1)
    for s in range(4):
        every = lax.dot_general(
            incoming_ref[s], held_ref[...], (((1,), (1,)), ((), ())), preferred_element_type=f32
        )
        products_ref[pl.ds(s * layers + layer, 1), :] = jnp.sum(jnp.where(same, every, 0.0), axis=0, keepdims=True)


def generate_kernel(
    parts_ref, weight_ref,
    mixing_ref, active_ref, slope_ref, preact_ref, factor_ref,
):
    hidden = weight_ref.shape[0]
    parts = parts_ref[...].astype(f32)
    packed = (parts[0] + parts[1]) + (parts[2] + parts[3])
    factor = lax.rsqrt(packed[:, hidden : hidden + 1] / D + epsilon)
    preact = factor * packed[:, :hidden]
    factor_ref[...] = jnp.broadcast_to(factor, factor_ref.shape)
    preact_ref[...] = preact
    inside = 0.7978845608028654 * (preact + 0.044715 * (preact * preact * preact))
    bent = jnp.tanh(inside)
    active = (0.5 * preact * (1.0 + bent)).astype(bf16)
    active_ref[...] = active
    slope_ref[...] = 0.5 * (1.0 + bent) + 0.5 * preact * (1.0 - bent * bent) * (
        0.7978845608028654 * (1.0 + 3 * 0.044715 * (preact * preact))
    )
    mixing_ref[...] = jnp.dot(active, weight_ref[...], preferred_element_type=f32)


def own_kernel(layers, place_ref, held_ref, incoming_ref, products_ref):
    products_ref[...] = jnp.zeros_like(products_ref)
    put_products(held_ref, incoming_ref, products_ref, place_ref[0], layers)


def depth_kernel(turn, chain, layers, place_ref, held_ref, incoming_ref, before_ref, products_ref):
    products_ref[...] = before_ref[...]

    @pl.when(place_ref[1] == chain)
    def _():
        put_products(held_ref, incoming_ref, products_ref, (place_ref[0] - (turn - 1)) & (layers - 1), layers)


def tiles(shape):
    return [(slice(r, r + 16), slice(at, at + LANES)) for r in range(0, shape[0], 16) for at in range(0, shape[1], LANES)]


def hop_kernel(turn, chain, layers, place_ref, held_ref, incoming_ref, mixing_ref, sent_ref):
    rising = place_ref[1] == chain

    @pl.when(rising)
    def _():
        sent_ref[...] = held_ref[...]

    @pl.when(jnp.logical_not(rising))
    def _():
        weights = weights_of(mixing_ref[...], place_ref[0] + turn - 1 - layers, layers)
        for rows, lanes in tiles(sent_ref.shape):
            total = add_term(rows, lanes, weights, incoming_ref, held_ref[rows, lanes].astype(f32))
            sent_ref[rows, lanes] = total.astype(bf16)


def finish_kernel(layers, place_ref, even_ref, odd_ref, incoming_ref, mixing_ref, generated_ref, out_ref):
    even = place_ref[1] == 0
    weights = weights_of(mixing_ref[...], place_ref[0], layers)
    for rows, lanes in tiles(out_ref.shape):
        came = jnp.where(even, odd_ref[rows, lanes].astype(f32), even_ref[rows, lanes].astype(f32))
        total = add_term(rows, lanes, weights, incoming_ref, came)
        out_ref[rows, lanes] = (total + generated_ref[rows, lanes]).astype(bf16)


def gradient_kernel(
    parts_ref, weight_ref, active_ref, slope_ref, preact_ref, factor_ref, turned_ref, local_ref, scaled_grad_ref, back_ref
):
    rows = turned_ref.shape[0] // SPREAD
    parts = parts_ref[...]
    products = (parts[0] + parts[1]) + (parts[2] + parts[3])
    depth_turned = products.astype(bf16)
    depth_grads = products.T.astype(bf16)
    dactive = jnp.dot(depth_grads, weight_ref[...], preferred_element_type=f32)
    dpreact = dactive * slope_ref[...]
    factor = factor_ref[...][:, :1]
    inner = jnp.sum(dpreact * preact_ref[...], axis=1, keepdims=True)
    back_ref[...] = jnp.broadcast_to(factor * factor * inner / D, back_ref.shape)
    scaled_grad = (dpreact * factor).astype(bf16)
    scaled_grad_ref[...] = scaled_grad
    second = jnp.dot(depth_turned, active_ref[...], preferred_element_type=f32).astype(bf16)
    half = second.shape[0] // 2
    for m in range(SPREAD):
        local_ref[m, :rows] = jnp.dot(
            turned_ref[m * rows : (m + 1) * rows], scaled_grad, preferred_element_type=f32
        ).astype(bf16)
        local_ref[m, rows:] = second[(m % 2) * half : (m % 2 + 1) * half]


def over_dp(local, chains):
    size = lax.axis_size("dp")
    groups = [[x * 4 + z * 2 + core for x in range(size // 4) for core in range(2)] for z in range(2)]
    arrived = lax.all_to_all(local, "dp", 0, 0, axis_index_groups=groups, tiled=True)
    mine = jnp.sum(arrived.astype(f32), axis=0).astype(bf16)
    mine, *chains = lax.optimization_barrier((mine, *chains))
    other = lax.ppermute(mine, "dp", [(i, i ^ 2) for i in range(size)])
    total = (mine.astype(f32) + other.astype(f32)).astype(bf16)
    spread = jnp.broadcast_to(total[None], local.shape)
    return lax.all_to_all(spread, "dp", 0, 0, axis_index_groups=groups, tiled=True), chains


def on_device(outputs, cotangents, gains, first_weight, second_weight):
    layers = lax.axis_size("pipe")
    section = lax.axis_index("pipe")
    size = lax.axis_size("dp")
    last = layers - 1
    current = outputs[0]
    incoming = cotangents[:, 0]
    tokens, width = current.shape
    hidden = first_weight.shape[2]
    columns = 4 * layers
    shape = jax.ShapeDtypeStruct
    place = jnp.stack([section, lax.axis_index("dp") & 1]).astype(jnp.int32)

    def hop(array, turn, chain):
        pairs = [(k * size + i, (k + 1) * size + i) for k in range(turn - 1, last) for i in range(chain, size, 2)]
        if turn > 1:
            pairs += [
                (k * size + i, (k - 1) * size + i) for k in range(layers + 1 - turn, layers) for i in range(1 - chain, size, 2)
            ]
        return lax.ppermute(array, ("pipe", "dp"), pairs)

    packed, scaled = call(
        project_kernel,
        [shape((4, tokens, hidden + 128), bf16), shape((tokens, width), bf16)],
        2 * tokens * width * hidden,
        4 * width * (tokens + hidden),
        count=3,
    )(current, gains, first_weight[0])
    scaled, current = lax.optimization_barrier((scaled, current))
    packed = lax.all_to_all(packed, "tensor", 0, 0, tiled=True)
    mixing, active, slope, preact, factor = call(
        generate_kernel,
        [
            shape((tokens, columns), f32),
            shape((tokens, hidden), bf16),
            shape((tokens, hidden), f32),
            shape((tokens, hidden), f32),
            shape((tokens, 128), f32),
        ],
        2 * tokens * hidden * columns,
        20 * tokens * hidden,
        count=2,
    )(packed, second_weight[0])
    [products] = call(
        functools.partial(own_kernel, layers),
        [shape((columns, tokens), f32)],
        8 * tokens * width,
        10 * tokens * width,
        smem=1,
        count=3,
    )(place, current, incoming)

    chains = [hop(current, 1, chain) for chain in range(2)]
    for turn in range(2, layers + 1):
        for chain in range(2):
            held = chains[chain]
            [sent] = call(
                functools.partial(hop_kernel, turn, chain, layers),
                [shape((tokens, width), bf16)],
                8 * tokens * width,
                12 * tokens * width,
                smem=1,
                count=4,
            )(place, held, incoming, mixing)
            chains[chain] = hop(sent, turn, chain)
            [products] = call(
                functools.partial(depth_kernel, turn, chain, layers),
                [shape((columns, tokens), f32)],
                8 * tokens * width,
                10 * tokens * width,
                smem=1,
                count=4,
            )(place, held, incoming, products)
        mixing, products = lax.optimization_barrier((mixing, products))

    spread = lax.all_to_all(jnp.broadcast_to(products[None], (4, columns, tokens)), "tensor", 0, 0, tiled=True)
    local, scaled_grad, back = call(
        gradient_kernel,
        [
            shape((SPREAD, width // SPREAD + columns // 2, hidden), bf16),
            shape((tokens, hidden), bf16),
            shape((tokens, 128), f32),
        ],
        2 * tokens * width * hidden,
        4 * width * (tokens + hidden),
        count=7,
    )(spread, second_weight[0].T, active, slope, preact, factor, scaled.T)
    summed, chains = over_dp(local, chains)
    summed = summed.astype(f32)
    divisor = tokens * size
    first_grads = summed[:, : width // SPREAD].reshape(width, hidden) / divisor
    second_grads = summed[:2, width // SPREAD :].reshape(columns, hidden).T / divisor

    weighted = lax.dot_general(scaled_grad, first_weight[0], (((1,), (1,)), ((), ())), preferred_element_type=f32)
    generated = weighted * gains[0].astype(f32)[None] - current.astype(f32) * back[:, :1]
    [output_grads] = call(
        functools.partial(finish_kernel, layers),
        [shape((tokens, width), bf16)],
        8 * tokens * width,
        16 * tokens * width,
        smem=1,
        count=6,
    )(place, chains[0], chains[1], incoming, mixing, generated)
    return (output_grads[None], first_grads[None], second_grads[None])


def solution(mesh):
    placed = (
        P("pipe", "dp", "tensor"),
        P(None, "pipe", "dp", "tensor"),
        P("pipe", "tensor"),
        P("pipe", "tensor", None),
        P("pipe", None, None),
    )
    return jax.shard_map(
        on_device,
        mesh=mesh,
        in_specs=placed,
        out_specs=(P("pipe", "dp", "tensor"), P("pipe", "tensor", None), P("pipe", None, None)),
        check_vma=False,
    )
```

```python
import functools

import jax
import jax.numpy as jnp
from jax import lax
from jax.experimental import pallas as pl
from jax.experimental.pallas import tpu as pltpu
from jax.sharding import PartitionSpec as P

D = 6144
epsilon = 1e-06
LAG = 2
LANES = 512

f32 = jnp.float32
bf16 = jnp.bfloat16


def call(kernel, shapes, flops, moved, scratch=(), smem=0, count=0):
    return pl.pallas_call(
        kernel,
        out_shape=shapes,
        in_specs=[pl.BlockSpec(memory_space=pltpu.SMEM)] * smem
        + [pl.BlockSpec(memory_space=pltpu.VMEM)] * (count - smem),
        out_specs=[pl.BlockSpec(memory_space=pltpu.VMEM)] * len(shapes),
        scratch_shapes=list(scratch),
        compiler_params=pltpu.CompilerParams(vmem_limit_bytes=20 * 1024 * 1024),
        cost_estimate=pl.CostEstimate(flops=flops, bytes_accessed=moved, transcendentals=0),
    )


def project_kernel(x_ref, gain_ref, weight_ref, packed_ref, turned_ref):
    hidden = weight_ref.shape[1]
    tokens = x_ref.shape[0]
    x = x_ref[...].astype(f32)
    scaled = (x * gain_ref[...].astype(f32)).astype(bf16)
    turned_ref[...] = scaled.astype(f32).T.astype(bf16)
    projected = jnp.dot(scaled, weight_ref[...], preferred_element_type=f32).astype(bf16)
    squares = jnp.broadcast_to(jnp.sum(x * x, axis=1, keepdims=True), (tokens, 128)).astype(bf16)
    for m in range(packed_ref.shape[0]):
        packed_ref[m, :, :hidden] = projected
        packed_ref[m, :, hidden:] = squares


def weights_of(mixed, layer, layers):
    lane = lax.broadcasted_iota(jnp.int32, mixed.shape, 1)
    return [
        jnp.sum(jnp.where(lane == jnp.where(layer < 0, -1, s * layers + layer), mixed, 0.0), axis=1, keepdims=True)
        for s in range(4)
    ]


def add_term(rows, lanes, weights, incoming_ref, total):
    for s in range(4):
        total = total + weights[s][rows] * incoming_ref[s, rows, lanes].astype(f32)
    return total


def put_products(held_ref, incoming_ref, products_ref, layer, layers):
    tokens = held_ref.shape[0]
    same = lax.broadcasted_iota(jnp.int32, (tokens, tokens), 0) == lax.broadcasted_iota(jnp.int32, (tokens, tokens), 1)
    for s in range(4):
        every = lax.dot_general(
            incoming_ref[s], held_ref[...], (((1,), (1,)), ((), ())), preferred_element_type=f32
        )
        products_ref[pl.ds(s * layers + layer, 1), :] = jnp.sum(jnp.where(same, every, 0.0), axis=0, keepdims=True)


def generate_kernel(
    parts_ref, weight_ref, scaled_ref,
    mixing_ref, slope_ref, preact_ref, factor_ref, payload_ref,
):
    hidden = weight_ref.shape[0]
    parts = parts_ref[...].astype(f32)
    packed = (parts[0] + parts[1]) + (parts[2] + parts[3])
    factor = lax.rsqrt(packed[:, hidden : hidden + 1] / D + epsilon)
    preact = factor * packed[:, :hidden]
    factor_ref[...] = jnp.broadcast_to(factor, factor_ref.shape)
    preact_ref[...] = preact
    inside = 0.7978845608028654 * (preact + 0.044715 * (preact * preact * preact))
    bent = jnp.tanh(inside)
    active = (0.5 * preact * (1.0 + bent)).astype(bf16)
    slope = 0.5 * (1.0 + bent) + 0.5 * preact * (1.0 - bent * bent) * (
        0.7978845608028654 * (1.0 + 3 * 0.044715 * (preact * preact))
    )
    slope_ref[...] = slope
    first = (slope * factor).T.astype(bf16)
    second = active.astype(f32).T.astype(bf16)
    members, chunk = payload_ref.shape[0], payload_ref.shape[1] - 2 * hidden
    for m in range(members):
        payload_ref[m, :chunk] = scaled_ref[m * chunk : (m + 1) * chunk]
        payload_ref[m, chunk : chunk + hidden] = first
        payload_ref[m, chunk + hidden :] = second
    mixing_ref[...] = jnp.dot(active, weight_ref[...], preferred_element_type=f32)


def own_kernel(layers, place_ref, held_ref, incoming_ref, products_ref):
    products_ref[...] = jnp.zeros_like(products_ref)

    @pl.when(place_ref[1] == 0)
    def _():
        put_products(held_ref, incoming_ref, products_ref, place_ref[0], layers)


def depth_kernel(turn, layers, place_ref, held_ref, incoming_ref, before_ref, products_ref):
    products_ref[...] = before_ref[...]

    @pl.when(place_ref[1] == 0)
    def _():
        put_products(held_ref, incoming_ref, products_ref, (place_ref[0] - (turn - 1)) & (layers - 1), layers)


def tiles(shape):
    return [(slice(r, r + 16), slice(at, at + LANES)) for r in range(0, shape[0], 16) for at in range(0, shape[1], LANES)]


def hop_kernel(turn, layers, place_ref, held_ref, incoming_ref, mixing_ref, sent_ref):
    rising = place_ref[1] == 0

    @pl.when(rising)
    def _():
        sent_ref[...] = held_ref[...]

    @pl.when(jnp.logical_not(rising))
    def _():
        weights = weights_of(mixing_ref[...], place_ref[0] + turn - LAG - layers, layers)
        for rows, lanes in tiles(sent_ref.shape):
            total = add_term(rows, lanes, weights, incoming_ref, held_ref[rows, lanes].astype(f32))
            sent_ref[rows, lanes] = total.astype(bf16)


def finish_kernel(layers, place_ref, given_ref, kept_ref, incoming_ref, mixing_ref, generated_ref, out_ref):
    even = place_ref[1] == 0
    weights = weights_of(mixing_ref[...], place_ref[0], layers)
    for rows, lanes in tiles(out_ref.shape):
        came = jnp.where(even, given_ref[rows, lanes].astype(f32), kept_ref[rows, lanes].astype(f32))
        total = add_term(rows, lanes, weights, incoming_ref, came)
        out_ref[rows, lanes] = (total + generated_ref[rows, lanes]).astype(bf16)


def depth_grad_kernel(parts_ref, spread_ref):
    parts = parts_ref[...]
    turned = ((parts[0] + parts[1]) + (parts[2] + parts[3])).astype(bf16)
    for m in range(spread_ref.shape[0]):
        spread_ref[m] = turned


def chunk_kernel(depth_ref, weight_ref, gathered_ref, mine_ref):
    hidden, columns = weight_ref.shape
    members, rows = gathered_ref.shape[0], gathered_ref.shape[1] - 2 * hidden
    first = jnp.zeros((rows, hidden), f32)
    second = jnp.zeros((columns, hidden), f32)
    across = (((1,), (1,)), ((), ()))
    for m in range(members):
        depth = depth_ref[m // 2 * 2, m % 2 * columns : (m % 2 + 1) * columns]
        dactive = jnp.dot(weight_ref[...], depth, preferred_element_type=f32)
        scaled_grad = (dactive * gathered_ref[m, rows : rows + hidden].astype(f32)).astype(bf16)
        first = first + lax.dot_general(gathered_ref[m, :rows], scaled_grad, across, preferred_element_type=f32)
        second = second + lax.dot_general(depth, gathered_ref[m, rows + hidden :], across, preferred_element_type=f32)
    mine_ref[:rows] = first.astype(bf16)
    mine_ref[rows:] = second.astype(bf16)


def gradient_kernel(place_ref, depth_ref, weight_ref, slope_ref, preact_ref, factor_ref, scaled_grad_ref, back_ref):
    both = depth_ref[place_ref[2]].astype(f32)
    columns = weight_ref.shape[0]
    depth_grads = jnp.where(place_ref[1] == 0, both[:columns], both[columns:]).T.astype(bf16)
    dactive = jnp.dot(depth_grads, weight_ref[...], preferred_element_type=f32)
    dpreact = dactive * slope_ref[...]
    factor = factor_ref[...][:, :1]
    inner = jnp.sum(dpreact * preact_ref[...], axis=1, keepdims=True)
    back_ref[...] = jnp.broadcast_to(factor * factor * inner / D, back_ref.shape)
    scaled_grad_ref[...] = (dpreact * factor).astype(bf16)


def on_device(outputs, cotangents, gains, first_weight, second_weight):
    layers = lax.axis_size("pipe")
    section = lax.axis_index("pipe")
    size = lax.axis_size("dp")
    last = layers - 1
    current = outputs[0]
    incoming = cotangents[:, 0]
    tokens, width = current.shape
    hidden = first_weight.shape[2]
    columns = 4 * layers
    shape = jax.ShapeDtypeStruct
    index = lax.axis_index("dp")
    even = lax.shift_right_logical(index, 2) * 2
    place = jnp.stack([section, index & 1, even]).astype(jnp.int32)
    members = size // 2
    chunk = width // members
    groups = [[x * 4 + z * 2 + core for x in range(size // 4) for core in range(2)] for z in range(2)]

    def swap(array):
        return lax.ppermute(array, "dp", [(i, i ^ 1) for i in range(size)])

    def hop(array, turn):
        pairs = [(k * size + i, (k + 1) * size + i) for k in range(turn - 1, last) for i in range(0, size, 2)]
        if turn > LAG:
            pairs += [(k * size + i, (k - 1) * size + i) for k in range(layers + LAG - turn, layers) for i in range(1, size, 2)]
        return lax.ppermute(array, ("pipe", "dp"), pairs)

    swapped, incoming = lax.optimization_barrier((swap(current), incoming))
    halves = [current, swapped]
    chains = [hop(halves[h], 1) for h in range(2)]
    across = swap(incoming)
    rising = [incoming, across]
    falling = [across, incoming]

    packed, scaled_turned = call(
        project_kernel,
        [shape((4, tokens, hidden + 128), bf16), shape((width, tokens), bf16)],
        2 * tokens * width * hidden,
        4 * width * (tokens + hidden),
        count=3,
    )(current, gains, first_weight[0])
    packed = lax.all_to_all(packed, "tensor", 0, 0, tiled=True)
    mixing, slope, preact, factor, payload = call(
        generate_kernel,
        [
            shape((tokens, columns), f32),
            shape((tokens, hidden), f32),
            shape((tokens, hidden), f32),
            shape((tokens, 128), f32),
            shape((members, chunk + 2 * hidden, tokens), bf16),
        ],
        2 * tokens * hidden * columns,
        20 * tokens * hidden,
        count=3,
    )(packed, second_weight[0], scaled_turned)
    mixings = [swap(mixing), mixing]
    products = [
        call(
            functools.partial(own_kernel, layers),
            [shape((columns, tokens), f32)],
            8 * tokens * width,
            10 * tokens * width,
            smem=1,
            count=3,
        )(place, halves[h], rising[h])[0]
        for h in range(2)
    ]

    def advance(turn, h):
        if turn <= LAG:
            return hop(chains[h], turn)
        [sent] = call(
            functools.partial(hop_kernel, turn, layers),
            [shape((tokens, width), bf16)],
            8 * tokens * width,
            12 * tokens * width,
            smem=1,
            count=4,
        )(place, chains[h], falling[h], mixings[h])
        return hop(sent, turn)

    for turn in range(2, layers + 1):
        for h in range(2):
            held = chains[h]
            chains[h] = advance(turn, h)
            [products[h]] = call(
                functools.partial(depth_kernel, turn, layers),
                [shape((columns, tokens), f32)],
                8 * tokens * width,
                10 * tokens * width,
                smem=1,
                count=4,
            )(place, held, rising[h], products[h])
        if turn == LAG:
            payload, *products = lax.optimization_barrier((payload, *products))
            gathered = lax.all_to_all(payload, "dp", 0, 0, axis_index_groups=groups, tiled=True)
        if turn == 2 * LAG:
            gathered, *products = lax.optimization_barrier((gathered, *products))
        *mixings, products[0], products[1] = lax.optimization_barrier((*mixings, *products))

    both = jnp.concatenate(products, axis=0)
    spread = lax.all_to_all(jnp.broadcast_to(both[None], (4, *both.shape)), "tensor", 0, 0, tiled=True)
    [depth_grads] = call(depth_grad_kernel, [shape((members, 2 * columns, tokens), bf16)], 0, 8 * columns * tokens, count=1)(spread)
    depth_all = lax.all_to_all(depth_grads, "dp", 0, 0, axis_index_groups=groups, tiled=True)
    [mine] = call(
        chunk_kernel,
        [shape((chunk + columns, hidden), bf16)],
        2 * tokens * width * hidden,
        4 * members * tokens * hidden,
        count=3,
    )(depth_all, second_weight[0], gathered)
    mine, *chains = lax.optimization_barrier((mine, *chains))
    other = lax.ppermute(mine, "dp", [(i, i ^ 2) for i in range(size)])
    for turn in range(layers + 1, layers + LAG):
        chains = [advance(turn, h) for h in range(2)]
    other, *chains = lax.optimization_barrier((other, *chains))
    total = mine.astype(f32) + other.astype(f32)
    divisor = tokens * size
    second_grads = total[chunk:].T / divisor
    spread = jnp.broadcast_to(total[None, :chunk].astype(bf16), (members, chunk, hidden))
    summed = lax.all_to_all(spread, "dp", 0, 0, axis_index_groups=groups, tiled=True)
    first_grads = summed.astype(f32).reshape(width, hidden) / divisor

    scaled_grad, back = call(
        gradient_kernel,
        [shape((tokens, hidden), bf16), shape((tokens, 128), f32)],
        2 * tokens * hidden * columns,
        16 * tokens * hidden,
        smem=1,
        count=6,
    )(place, depth_all, second_weight[0].T, slope, preact, factor)

    weighted = lax.dot_general(scaled_grad, first_weight[0], (((1,), (1,)), ((), ())), preferred_element_type=f32)
    generated = weighted * gains[0].astype(f32)[None] - current.astype(f32) * back[:, :1]
    given = lax.ppermute(chains[0], "dp", [(i, i ^ 1) for i in range(1, size, 2)])
    [output_grads] = call(
        functools.partial(finish_kernel, layers),
        [shape((tokens, width), bf16)],
        8 * tokens * width,
        16 * tokens * width,
        smem=1,
        count=6,
    )(place, given, chains[1], incoming, mixing, generated)
    return (output_grads[None], first_grads[None], second_grads[None])


def solution(mesh):
    placed = (
        P("pipe", "dp", "tensor"),
        P(None, "pipe", "dp", "tensor"),
        P("pipe", "tensor"),
        P("pipe", "tensor", None),
        P("pipe", None, None),
    )
    return jax.shard_map(
        on_device,
        mesh=mesh,
        in_specs=placed,
        out_specs=(P("pipe", "dp", "tensor"), P("pipe", "tensor", None), P("pipe", None, None)),
        check_vma=False,
    )
```

```python
import functools

import jax
import jax.numpy as jnp
from jax import lax
from jax.experimental import pallas as pl
from jax.experimental.pallas import tpu as pltpu
from jax.sharding import PartitionSpec as P

D = 6144
epsilon = 1e-06
LAG = 2
LANES = 512

f32 = jnp.float32
bf16 = jnp.bfloat16


def call(kernel, shapes, flops, moved, scratch=(), smem=0, count=0):
    return pl.pallas_call(
        kernel,
        out_shape=shapes,
        in_specs=[pl.BlockSpec(memory_space=pltpu.SMEM)] * smem
        + [pl.BlockSpec(memory_space=pltpu.VMEM)] * (count - smem),
        out_specs=[pl.BlockSpec(memory_space=pltpu.VMEM)] * len(shapes),
        scratch_shapes=list(scratch),
        compiler_params=pltpu.CompilerParams(vmem_limit_bytes=6 * 1024 * 1024),
        cost_estimate=pl.CostEstimate(flops=flops, bytes_accessed=moved, transcendentals=0),
    )


def project_kernel(x_ref, gain_ref, weight_ref, packed_ref, turned_ref):
    hidden = weight_ref.shape[1]
    tokens = x_ref.shape[0]
    x = x_ref[...].astype(f32)
    scaled = (x * gain_ref[...].astype(f32)).astype(bf16)
    turned_ref[...] = scaled.astype(f32).T.astype(bf16)
    projected = jnp.dot(scaled, weight_ref[...], preferred_element_type=f32).astype(bf16)
    squares = jnp.broadcast_to(jnp.sum(x * x, axis=1, keepdims=True), (tokens, 128)).astype(bf16)
    for m in range(packed_ref.shape[0]):
        packed_ref[m, :, :hidden] = projected
        packed_ref[m, :, hidden:] = squares


def weights_of(mixed, layer, layers):
    lane = lax.broadcasted_iota(jnp.int32, mixed.shape, 1)
    return [
        jnp.sum(jnp.where(lane == jnp.where(layer < 0, -1, s * layers + layer), mixed, 0.0), axis=1, keepdims=True)
        for s in range(4)
    ]


def add_term(rows, lanes, weights, incoming_ref, total):
    for s in range(4):
        total = total + weights[s][rows] * incoming_ref[s, rows, lanes].astype(f32)
    return total


def put_products(held_ref, incoming_ref, products_ref, start, layers):
    tokens = held_ref.shape[0]
    same = lax.broadcasted_iota(jnp.int32, (tokens, tokens), 0) == lax.broadcasted_iota(jnp.int32, (tokens, tokens), 1)
    for s in range(4):
        every = lax.dot_general(
            incoming_ref[s], held_ref[...], (((1,), (1,)), ((), ())), preferred_element_type=f32
        )
        products_ref[pl.ds(start + s * layers, 1), :] = jnp.sum(jnp.where(same, every, 0.0), axis=0, keepdims=True)


def generate_kernel(
    parts_ref, weight_ref, scaled_ref,
    mixing_ref, slope_ref, preact_ref, factor_ref, payload_ref,
):
    hidden = weight_ref.shape[0]
    parts = parts_ref[...].astype(f32)
    packed = (parts[0] + parts[1]) + (parts[2] + parts[3])
    factor = lax.rsqrt(packed[:, hidden : hidden + 1] / D + epsilon)
    preact = factor * packed[:, :hidden]
    factor_ref[...] = jnp.broadcast_to(factor, factor_ref.shape)
    preact_ref[...] = preact
    inside = 0.7978845608028654 * (preact + 0.044715 * (preact * preact * preact))
    bent = jnp.tanh(inside)
    active = (0.5 * preact * (1.0 + bent)).astype(bf16)
    slope = 0.5 * (1.0 + bent) + 0.5 * preact * (1.0 - bent * bent) * (
        0.7978845608028654 * (1.0 + 3 * 0.044715 * (preact * preact))
    )
    slope_ref[...] = slope
    first = (slope * factor).T.astype(bf16)
    second = active.astype(f32).T.astype(bf16)
    members, chunk = payload_ref.shape[0], payload_ref.shape[1] - 2 * hidden
    for m in range(members):
        payload_ref[m, :chunk] = scaled_ref[m * chunk : (m + 1) * chunk]
        payload_ref[m, chunk : chunk + hidden] = first
        payload_ref[m, chunk + hidden :] = second
    mixing_ref[...] = jnp.dot(active, weight_ref[...], preferred_element_type=f32)


def own_kernel(layers, place_ref, even_ref, odd_ref, even_in_ref, odd_in_ref, products_ref):
    products_ref[...] = jnp.zeros_like(products_ref)

    @pl.when(place_ref[1] == 0)
    def _():
        put_products(even_ref, even_in_ref, products_ref, place_ref[0], layers)
        put_products(odd_ref, odd_in_ref, products_ref, 4 * layers + place_ref[0], layers)


def depth_kernel(turn, layers, place_ref, even_ref, odd_ref, even_in_ref, odd_in_ref, before_ref, products_ref):
    products_ref[...] = before_ref[...]

    @pl.when(place_ref[1] == 0)
    def _():
        layer = (place_ref[0] - (turn - 1)) & (layers - 1)
        put_products(even_ref, even_in_ref, products_ref, layer, layers)
        put_products(odd_ref, odd_in_ref, products_ref, 4 * layers + layer, layers)


def tiles(shape):
    return [(slice(r, r + 16), slice(at, at + LANES)) for r in range(0, shape[0], 16) for at in range(0, shape[1], LANES)]


def hop_kernel(turn, layers, place_ref, held_ref, incoming_ref, mixing_ref, sent_ref):
    rising = place_ref[1] == 0

    @pl.when(rising)
    def _():
        sent_ref[...] = held_ref[...]

    @pl.when(jnp.logical_not(rising))
    def _():
        weights = weights_of(mixing_ref[...], place_ref[0] + turn - LAG - layers, layers)
        for rows, lanes in tiles(sent_ref.shape):
            total = add_term(rows, lanes, weights, incoming_ref, held_ref[rows, lanes].astype(f32))
            sent_ref[rows, lanes] = total.astype(bf16)


def finish_kernel(layers, place_ref, given_ref, kept_ref, incoming_ref, mixing_ref, generated_ref, out_ref):
    even = place_ref[1] == 0
    weights = weights_of(mixing_ref[...], place_ref[0], layers)
    for rows, lanes in tiles(out_ref.shape):
        came = jnp.where(even, given_ref[rows, lanes].astype(f32), kept_ref[rows, lanes].astype(f32))
        total = add_term(rows, lanes, weights, incoming_ref, came)
        out_ref[rows, lanes] = (total + generated_ref[rows, lanes]).astype(bf16)


def depth_grad_kernel(parts_ref, spread_ref):
    parts = parts_ref[...]
    turned = ((parts[0] + parts[1]) + (parts[2] + parts[3])).astype(bf16)
    for m in range(spread_ref.shape[0]):
        spread_ref[m] = turned


def chunk_kernel(depth_ref, weight_ref, gathered_ref, mine_ref):
    hidden, columns = weight_ref.shape
    members, rows = gathered_ref.shape[0], gathered_ref.shape[1] - 2 * hidden
    first = jnp.zeros((rows, hidden), f32)
    second = jnp.zeros((columns, hidden), f32)
    across = (((1,), (1,)), ((), ()))
    for m in range(members):
        depth = depth_ref[m // 2 * 2, m % 2 * columns : (m % 2 + 1) * columns]
        dactive = jnp.dot(weight_ref[...], depth, preferred_element_type=f32)
        scaled_grad = (dactive * gathered_ref[m, rows : rows + hidden].astype(f32)).astype(bf16)
        first = first + lax.dot_general(gathered_ref[m, :rows], scaled_grad, across, preferred_element_type=f32)
        second = second + lax.dot_general(depth, gathered_ref[m, rows + hidden :], across, preferred_element_type=f32)
    mine_ref[:rows] = first.astype(bf16)
    mine_ref[rows:] = second.astype(bf16)


def gradient_kernel(place_ref, depth_ref, weight_ref, slope_ref, preact_ref, factor_ref, scaled_grad_ref, back_ref):
    both = depth_ref[place_ref[2]].astype(f32)
    columns = weight_ref.shape[0]
    depth_grads = jnp.where(place_ref[1] == 0, both[:columns], both[columns:]).T.astype(bf16)
    dactive = jnp.dot(depth_grads, weight_ref[...], preferred_element_type=f32)
    dpreact = dactive * slope_ref[...]
    factor = factor_ref[...][:, :1]
    inner = jnp.sum(dpreact * preact_ref[...], axis=1, keepdims=True)
    back_ref[...] = jnp.broadcast_to(factor * factor * inner / D, back_ref.shape)
    scaled_grad_ref[...] = (dpreact * factor).astype(bf16)


def on_device(outputs, cotangents, gains, first_weight, second_weight):
    layers = lax.axis_size("pipe")
    section = lax.axis_index("pipe")
    size = lax.axis_size("dp")
    last = layers - 1
    current = outputs[0]
    incoming = cotangents[:, 0]
    tokens, width = current.shape
    hidden = first_weight.shape[2]
    columns = 4 * layers
    shape = jax.ShapeDtypeStruct
    index = lax.axis_index("dp")
    even = lax.shift_right_logical(index, 2) * 2
    place = jnp.stack([section, index & 1, even]).astype(jnp.int32)
    members = size // 2
    chunk = width // members
    groups = [[x * 4 + z * 2 + core for x in range(size // 4) for core in range(2)] for z in range(2)]

    def swap(array):
        return lax.ppermute(array, "dp", [(i, i ^ 1) for i in range(size)])

    def hop(array, turn):
        pairs = [(k * size + i, (k + 1) * size + i) for k in range(turn - 1, last) for i in range(0, size, 2)]
        if turn > LAG:
            pairs += [(k * size + i, (k - 1) * size + i) for k in range(layers + LAG - turn, layers) for i in range(1, size, 2)]
        return lax.ppermute(array, ("pipe", "dp"), pairs)

    halves = [current, swap(current)]
    chains = [hop(halves[h], 1) for h in range(2)]

    packed, scaled_turned = call(
        project_kernel,
        [shape((4, tokens, hidden + 128), bf16), shape((width, tokens), bf16)],
        2 * tokens * width * hidden,
        4 * width * (tokens + hidden),
        count=3,
    )(current, gains, first_weight[0])
    packed = lax.all_to_all(packed, "tensor", 0, 0, tiled=True)
    scaled_turned, incoming, *chains = lax.optimization_barrier((scaled_turned, incoming, *chains))
    across = swap(incoming)
    rising = [incoming, across]
    falling = [across, incoming]
    early = [hop(chains[h], LAG) for h in range(2)]
    packed, *early = lax.optimization_barrier((packed, *early))
    mixing, slope, preact, factor, payload = call(
        generate_kernel,
        [
            shape((tokens, columns), f32),
            shape((tokens, hidden), f32),
            shape((tokens, hidden), f32),
            shape((tokens, 128), f32),
            shape((members, chunk + 2 * hidden, tokens), bf16),
        ],
        2 * tokens * hidden * columns,
        20 * tokens * hidden,
        count=3,
    )(packed, second_weight[0], scaled_turned)
    mixings = [swap(mixing), mixing]
    [products] = call(
        functools.partial(own_kernel, layers),
        [shape((2 * columns, tokens), f32)],
        16 * tokens * width,
        20 * tokens * width,
        smem=1,
        count=5,
    )(place, *halves, *rising)

    def advance(turn, h):
        [sent] = call(
            functools.partial(hop_kernel, turn, layers),
            [shape((tokens, width), bf16)],
            8 * tokens * width,
            12 * tokens * width,
            smem=1,
            count=4,
        )(place, chains[h], falling[h], mixings[h])
        return hop(sent, turn)

    for turn in range(2, layers + 1):
        held = chains
        chains = early if turn == LAG else [advance(turn, h) for h in range(2)]
        [products] = call(
            functools.partial(depth_kernel, turn, layers),
            [shape((2 * columns, tokens), f32)],
            16 * tokens * width,
            20 * tokens * width,
            smem=1,
            count=6,
        )(place, *held, *rising, products)
        if turn == LAG:
            payload, products = lax.optimization_barrier((payload, products))
            gathered = lax.all_to_all(payload, "dp", 0, 0, axis_index_groups=groups, tiled=True)
        if turn == 2 * LAG:
            gathered, products = lax.optimization_barrier((gathered, products))
        *mixings, products = lax.optimization_barrier((*mixings, products))

    spread = lax.all_to_all(jnp.broadcast_to(products[None], (4, *products.shape)), "tensor", 0, 0, tiled=True)
    [depth_grads] = call(depth_grad_kernel, [shape((members, 2 * columns, tokens), bf16)], 0, 8 * columns * tokens, count=1)(spread)
    depth_all = lax.all_to_all(depth_grads, "dp", 0, 0, axis_index_groups=groups, tiled=True)
    [mine] = call(
        chunk_kernel,
        [shape((chunk + columns, hidden), bf16)],
        2 * tokens * width * hidden,
        4 * members * tokens * hidden,
        count=3,
    )(depth_all, second_weight[0], gathered)
    mine, *chains = lax.optimization_barrier((mine, *chains))
    other = lax.ppermute(mine, "dp", [(i, i ^ 2) for i in range(size)])
    total = mine.astype(f32) + other.astype(f32)
    divisor = tokens * size
    second_grads = total[chunk:].T / divisor
    spread = jnp.broadcast_to(total[None, :chunk].astype(bf16), (size // 4, chunk, hidden))
    along = [[x * 4 + rest for x in range(size // 4)] for rest in range(4)]
    for turn in range(layers + 1, layers + LAG):
        chains = [advance(turn, h) for h in range(2)]
    own = lax.all_to_all(spread, "dp", 0, 0, axis_index_groups=along, tiled=True)
    own, *chains = lax.optimization_barrier((own, *chains))
    far = swap(own)
    near = (index & 1) == 0
    summed = jnp.stack([jnp.where(near, own, far), jnp.where(near, far, own)], axis=1)
    first_grads = summed.astype(f32).reshape(width, hidden) / divisor

    scaled_grad, back = call(
        gradient_kernel,
        [shape((tokens, hidden), bf16), shape((tokens, 128), f32)],
        2 * tokens * hidden * columns,
        16 * tokens * hidden,
        smem=1,
        count=6,
    )(place, depth_all, second_weight[0].T, slope, preact, factor)

    weighted = lax.dot_general(scaled_grad, first_weight[0], (((1,), (1,)), ((), ())), preferred_element_type=f32)
    generated = weighted * gains[0].astype(f32)[None] - current.astype(f32) * back[:, :1]
    given = lax.ppermute(chains[0], "dp", [(i, i ^ 1) for i in range(1, size, 2)])
    [output_grads] = call(
        functools.partial(finish_kernel, layers),
        [shape((tokens, width), bf16)],
        8 * tokens * width,
        16 * tokens * width,
        smem=1,
        count=6,
    )(place, given, chains[1], incoming, mixing, generated)
    return (output_grads[None], first_grads[None], second_grads[None])


def solution(mesh):
    placed = (
        P("pipe", "dp", "tensor"),
        P(None, "pipe", "dp", "tensor"),
        P("pipe", "tensor"),
        P("pipe", "tensor", None),
        P("pipe", None, None),
    )
    return jax.shard_map(
        on_device,
        mesh=mesh,
        in_specs=placed,
        out_specs=(P("pipe", "dp", "tensor"), P("pipe", "tensor", None), P("pipe", None, None)),
        check_vma=False,
    )
```

```python
import functools

import jax
import jax.numpy as jnp
from jax import lax
from jax.experimental import pallas as pl
from jax.experimental.pallas import tpu as pltpu
from jax.sharding import PartitionSpec as P

D = 6144
epsilon = 1e-06
LAG = 2
LANES = 512

f32 = jnp.float32
bf16 = jnp.bfloat16


def call(kernel, shapes, flops, moved, scratch=(), smem=0, count=0):
    return pl.pallas_call(
        kernel,
        out_shape=shapes,
        in_specs=[pl.BlockSpec(memory_space=pltpu.SMEM)] * smem
        + [pl.BlockSpec(memory_space=pltpu.VMEM)] * (count - smem),
        out_specs=[pl.BlockSpec(memory_space=pltpu.VMEM)] * len(shapes),
        scratch_shapes=list(scratch),
        compiler_params=pltpu.CompilerParams(vmem_limit_bytes=20 * 1024 * 1024),
        cost_estimate=pl.CostEstimate(flops=flops, bytes_accessed=moved, transcendentals=0),
    )


def project_kernel(x_ref, gain_ref, weight_ref, packed_ref, turned_ref):
    hidden = weight_ref.shape[1]
    tokens = x_ref.shape[0]
    x = x_ref[...].astype(f32)
    scaled = (x * gain_ref[...].astype(f32)).astype(bf16)
    turned_ref[...] = scaled.astype(f32).T.astype(bf16)
    projected = jnp.dot(scaled, weight_ref[...], preferred_element_type=f32).astype(bf16)
    squares = jnp.broadcast_to(jnp.sum(x * x, axis=1, keepdims=True), (tokens, 128)).astype(bf16)
    for m in range(packed_ref.shape[0]):
        packed_ref[m, :, :hidden] = projected
        packed_ref[m, :, hidden:] = squares


def weights_of(mixed, layer, layers):
    lane = lax.broadcasted_iota(jnp.int32, mixed.shape, 1)
    return [
        jnp.sum(jnp.where(lane == jnp.where(layer < 0, -1, s * layers + layer), mixed, 0.0), axis=1, keepdims=True)
        for s in range(4)
    ]


def add_term(rows, lanes, weights, incoming_ref, total):
    for s in range(4):
        total = total + weights[s][rows] * incoming_ref[s, rows, lanes].astype(f32)
    return total


def put_products(held_ref, incoming_ref, products_ref, layer, layers):
    tokens = held_ref.shape[0]
    same = lax.broadcasted_iota(jnp.int32, (tokens, tokens), 0) == lax.broadcasted_iota(jnp.int32, (tokens, tokens), 1)
    for s in range(4):
        every = lax.dot_general(
            incoming_ref[s], held_ref[...], (((1,), (1,)), ((), ())), preferred_element_type=f32
        )
        products_ref[pl.ds(s * layers + layer, 1), :] = jnp.sum(jnp.where(same, every, 0.0), axis=0, keepdims=True)


def generate_kernel(
    parts_ref, weight_ref, scaled_ref,
    mixing_ref, slope_ref, preact_ref, factor_ref, payload_ref,
):
    hidden = weight_ref.shape[0]
    parts = parts_ref[...].astype(f32)
    packed = (parts[0] + parts[1]) + (parts[2] + parts[3])
    factor = lax.rsqrt(packed[:, hidden : hidden + 1] / D + epsilon)
    preact = factor * packed[:, :hidden]
    factor_ref[...] = jnp.broadcast_to(factor, factor_ref.shape)
    preact_ref[...] = preact
    inside = 0.7978845608028654 * (preact + 0.044715 * (preact * preact * preact))
    bent = jnp.tanh(inside)
    active = (0.5 * preact * (1.0 + bent)).astype(bf16)
    slope = 0.5 * (1.0 + bent) + 0.5 * preact * (1.0 - bent * bent) * (
        0.7978845608028654 * (1.0 + 3 * 0.044715 * (preact * preact))
    )
    slope_ref[...] = slope
    first = (slope * factor).T.astype(bf16)
    second = active.astype(f32).T.astype(bf16)
    members, chunk = payload_ref.shape[0], payload_ref.shape[1] - 2 * hidden
    for m in range(members):
        payload_ref[m, :chunk] = scaled_ref[m * chunk : (m + 1) * chunk]
        payload_ref[m, chunk : chunk + hidden] = first
        payload_ref[m, chunk + hidden :] = second
    mixing_ref[...] = jnp.dot(active, weight_ref[...], preferred_element_type=f32)


def own_kernel(layers, place_ref, held_ref, incoming_ref, products_ref):
    products_ref[...] = jnp.zeros_like(products_ref)
    put_products(held_ref, incoming_ref, products_ref, place_ref[0], layers)


def depth_kernel(turn, layers, place_ref, even_ref, odd_ref, incoming_ref, before_ref, products_ref):
    products_ref[...] = before_ref[...]
    layer = (place_ref[0] - (turn - 1)) & (layers - 1)
    for chain, held_ref in enumerate((even_ref, odd_ref)):

        @pl.when(place_ref[1] == chain)
        def _():
            put_products(held_ref, incoming_ref, products_ref, layer, layers)


def tiles(shape):
    return [(slice(r, r + 16), slice(at, at + LANES)) for r in range(0, shape[0], 16) for at in range(0, shape[1], LANES)]


def hop_kernel(turn, chain, layers, place_ref, held_ref, incoming_ref, mixing_ref, sent_ref):
    rising = place_ref[1] == chain

    @pl.when(rising)
    def _():
        sent_ref[...] = held_ref[...]

    @pl.when(jnp.logical_not(rising))
    def _():
        weights = weights_of(mixing_ref[...], place_ref[0] + turn - LAG - layers, layers)
        for rows, lanes in tiles(sent_ref.shape):
            total = add_term(rows, lanes, weights, incoming_ref, held_ref[rows, lanes].astype(f32))
            sent_ref[rows, lanes] = total.astype(bf16)


def finish_kernel(layers, place_ref, even_ref, odd_ref, incoming_ref, mixing_ref, generated_ref, out_ref):
    even = place_ref[1] == 0
    weights = weights_of(mixing_ref[...], place_ref[0], layers)
    for rows, lanes in tiles(out_ref.shape):
        came = jnp.where(even, odd_ref[rows, lanes].astype(f32), even_ref[rows, lanes].astype(f32))
        total = add_term(rows, lanes, weights, incoming_ref, came)
        out_ref[rows, lanes] = (total + generated_ref[rows, lanes]).astype(bf16)


def depth_grad_kernel(parts_ref, spread_ref):
    parts = parts_ref[...]
    turned = ((parts[0] + parts[1]) + (parts[2] + parts[3])).astype(bf16)
    for m in range(spread_ref.shape[0]):
        spread_ref[m] = turned


def chunk_kernel(depth_ref, weight_ref, gathered_ref, mine_ref):
    hidden = weight_ref.shape[0]
    members, rows = gathered_ref.shape[0], gathered_ref.shape[1] - 2 * hidden
    first = jnp.zeros((rows, hidden), f32)
    second = jnp.zeros((depth_ref.shape[1], hidden), f32)
    across = (((1,), (1,)), ((), ()))
    for m in range(members):
        depth = depth_ref[m]
        dactive = jnp.dot(weight_ref[...], depth, preferred_element_type=f32)
        scaled_grad = (dactive * gathered_ref[m, rows : rows + hidden].astype(f32)).astype(bf16)
        first = first + lax.dot_general(gathered_ref[m, :rows], scaled_grad, across, preferred_element_type=f32)
        second = second + lax.dot_general(depth, gathered_ref[m, rows + hidden :], across, preferred_element_type=f32)
    mine_ref[:rows] = first.astype(bf16)
    mine_ref[rows:] = second.astype(bf16)


def gradient_kernel(depth_ref, weight_ref, slope_ref, preact_ref, factor_ref, scaled_grad_ref, back_ref):
    depth_grads = depth_ref[0].astype(f32).T.astype(bf16)
    dactive = jnp.dot(depth_grads, weight_ref[...], preferred_element_type=f32)
    dpreact = dactive * slope_ref[...]
    factor = factor_ref[...][:, :1]
    inner = jnp.sum(dpreact * preact_ref[...], axis=1, keepdims=True)
    back_ref[...] = jnp.broadcast_to(factor * factor * inner / D, back_ref.shape)
    scaled_grad_ref[...] = (dpreact * factor).astype(bf16)


def on_device(outputs, cotangents, gains, first_weight, second_weight):
    layers = lax.axis_size("pipe")
    section = lax.axis_index("pipe")
    size = lax.axis_size("dp")
    last = layers - 1
    current = outputs[0]
    incoming = cotangents[:, 0]
    tokens, width = current.shape
    hidden = first_weight.shape[2]
    columns = 4 * layers
    shape = jax.ShapeDtypeStruct
    place = jnp.stack([section, lax.axis_index("dp") & 1]).astype(jnp.int32)

    def hop(array, turn, chain):
        pairs = [(k * size + i, (k + 1) * size + i) for k in range(turn - 1, last) for i in range(chain, size, 2)]
        if turn > LAG:
            pairs += [
                (k * size + i, (k - 1) * size + i) for k in range(layers + LAG - turn, layers) for i in range(1 - chain, size, 2)
            ]
        return lax.ppermute(array, ("pipe", "dp"), pairs)

    groups = [[x * 4 + z * 2 + core for x in range(size // 4) for core in range(2)] for z in range(2)]
    members = size // 2
    index = lax.axis_index("dp")
    chunk = width // members

    packed, scaled_turned = call(
        project_kernel,
        [shape((4, tokens, hidden + 128), bf16), shape((width, tokens), bf16)],
        2 * tokens * width * hidden,
        4 * width * (tokens + hidden),
        count=3,
    )(current, gains, first_weight[0])
    packed = lax.all_to_all(packed, "tensor", 0, 0, tiled=True)
    chains = [hop(current, 1, chain) for chain in range(2)]
    packed, *chains = lax.optimization_barrier((packed, *chains))
    mixing, slope, preact, factor, payload = call(
        generate_kernel,
        [
            shape((tokens, columns), f32),
            shape((tokens, hidden), f32),
            shape((tokens, hidden), f32),
            shape((tokens, 128), f32),
            shape((members, chunk + 2 * hidden, tokens), bf16),
        ],
        2 * tokens * hidden * columns,
        20 * tokens * hidden,
        count=3,
    )(packed, second_weight[0], scaled_turned)
    [products] = call(
        functools.partial(own_kernel, layers),
        [shape((columns, tokens), f32)],
        8 * tokens * width,
        10 * tokens * width,
        smem=1,
        count=3,
    )(place, current, incoming)

    def advance(turn, chain):
        if turn <= LAG:
            return hop(chains[chain], turn, chain)
        [sent] = call(
            functools.partial(hop_kernel, turn, chain, layers),
            [shape((tokens, width), bf16)],
            8 * tokens * width,
            12 * tokens * width,
            smem=1,
            count=4,
        )(place, chains[chain], incoming, mixing)
        return hop(sent, turn, chain)

    for turn in range(2, layers + 1):
        held = chains
        chains = [advance(turn, chain) for chain in range(2)]
        [products] = call(
            functools.partial(depth_kernel, turn, layers),
            [shape((columns, tokens), f32)],
            8 * tokens * width,
            10 * tokens * width,
            smem=1,
            count=5,
        )(place, *held, incoming, products)
        if turn == LAG:
            payload, products = lax.optimization_barrier((payload, products))
            gathered = lax.all_to_all(payload, "dp", 0, 0, axis_index_groups=groups, tiled=True)
        if turn == 2 * LAG:
            gathered, products = lax.optimization_barrier((gathered, products))
        mixing, products = lax.optimization_barrier((mixing, products))

    spread = lax.all_to_all(jnp.broadcast_to(products[None], (4, columns, tokens)), "tensor", 0, 0, tiled=True)
    [depth_grads] = call(depth_grad_kernel, [shape((members, columns, tokens), bf16)], 0, 8 * columns * tokens, count=1)(spread)
    depth_all = lax.all_to_all(depth_grads, "dp", 0, 0, axis_index_groups=groups, tiled=True)
    [mine] = call(
        chunk_kernel,
        [shape((chunk + columns, hidden), bf16)],
        2 * tokens * width * hidden,
        4 * members * tokens * hidden,
        count=3,
    )(depth_all, second_weight[0], gathered)
    mine, *chains = lax.optimization_barrier((mine, *chains))
    other = lax.ppermute(mine, "dp", [(i, i ^ 2) for i in range(size)])
    total = mine.astype(f32) + other.astype(f32)
    divisor = tokens * size
    second_grads = total[chunk:].T / divisor
    spread = jnp.broadcast_to(total[None, :chunk].astype(bf16), (size // 4, chunk, hidden))
    along = [[x * 4 + rest for x in range(size // 4)] for rest in range(4)]
    for turn in range(layers + 1, layers + LAG):
        chains = [advance(turn, chain) for chain in range(2)]
    own = lax.all_to_all(spread, "dp", 0, 0, axis_index_groups=along, tiled=True)
    own, *chains = lax.optimization_barrier((own, *chains))
    far = lax.ppermute(own, "dp", [(i, i ^ 1) for i in range(size)])
    near = (index & 1) == 0
    summed = jnp.stack([jnp.where(near, own, far), jnp.where(near, far, own)], axis=1)
    first_grads = summed.astype(f32).reshape(width, hidden) / divisor

    scaled_grad, back = call(
        gradient_kernel,
        [shape((tokens, hidden), bf16), shape((tokens, 128), f32)],
        2 * tokens * hidden * columns,
        16 * tokens * hidden,
        count=5,
    )(depth_grads, second_weight[0].T, slope, preact, factor)

    weighted = lax.dot_general(scaled_grad, first_weight[0], (((1,), (1,)), ((), ())), preferred_element_type=f32)
    generated = weighted * gains[0].astype(f32)[None] - current.astype(f32) * back[:, :1]
    [output_grads] = call(
        functools.partial(finish_kernel, layers),
        [shape((tokens, width), bf16)],
        8 * tokens * width,
        16 * tokens * width,
        smem=1,
        count=6,
    )(place, chains[0], chains[1], incoming, mixing, generated)
    return (output_grads[None], first_grads[None], second_grads[None])


def solution(mesh):
    placed = (
        P("pipe", "dp", "tensor"),
        P(None, "pipe", "dp", "tensor"),
        P("pipe", "tensor"),
        P("pipe", "tensor", None),
        P("pipe", None, None),
    )
    return jax.shard_map(
        on_device,
        mesh=mesh,
        in_specs=placed,
        out_specs=(P("pipe", "dp", "tensor"), P("pipe", "tensor", None), P("pipe", None, None)),
        check_vma=False,
    )
```

```python
import functools

import jax
import jax.numpy as jnp
from jax import lax
from jax.experimental import pallas as pl
from jax.experimental.pallas import tpu as pltpu
from jax.sharding import PartitionSpec as P

D = 6144
epsilon = 1e-06
LAG = 2
LANES = 512

f32 = jnp.float32
bf16 = jnp.bfloat16


def call(kernel, shapes, flops, moved, scratch=(), smem=0, count=0):
    return pl.pallas_call(
        kernel,
        out_shape=shapes,
        in_specs=[pl.BlockSpec(memory_space=pltpu.SMEM)] * smem
        + [pl.BlockSpec(memory_space=pltpu.VMEM)] * (count - smem),
        out_specs=[pl.BlockSpec(memory_space=pltpu.VMEM)] * len(shapes),
        scratch_shapes=list(scratch),
        compiler_params=pltpu.CompilerParams(vmem_limit_bytes=20 * 1024 * 1024),
        cost_estimate=pl.CostEstimate(flops=flops, bytes_accessed=moved, transcendentals=0),
    )


def project_kernel(x_ref, gain_ref, weight_ref, packed_ref, turned_ref):
    hidden = weight_ref.shape[1]
    tokens = x_ref.shape[0]
    x = x_ref[...].astype(f32)
    scaled = (x * gain_ref[...].astype(f32)).astype(bf16)
    turned_ref[...] = scaled.astype(f32).T.astype(bf16)
    projected = jnp.dot(scaled, weight_ref[...], preferred_element_type=f32).astype(bf16)
    squares = jnp.broadcast_to(jnp.sum(x * x, axis=1, keepdims=True), (tokens, 128)).astype(bf16)
    for m in range(packed_ref.shape[0]):
        packed_ref[m, :, :hidden] = projected
        packed_ref[m, :, hidden:] = squares


def weights_of(mixed, layer, layers):
    lane = lax.broadcasted_iota(jnp.int32, mixed.shape, 1)
    return [
        jnp.sum(jnp.where(lane == jnp.where(layer < 0, -1, s * layers + layer), mixed, 0.0), axis=1, keepdims=True)
        for s in range(4)
    ]


def add_term(rows, lanes, weights, incoming_ref, total):
    for s in range(4):
        total = total + weights[s][rows] * incoming_ref[s, rows, lanes].astype(f32)
    return total


def put_products(held_ref, incoming_ref, products_ref, layer, layers):
    tokens = held_ref.shape[0]
    same = lax.broadcasted_iota(jnp.int32, (tokens, tokens), 0) == lax.broadcasted_iota(jnp.int32, (tokens, tokens), 1)
    for s in range(4):
        every = lax.dot_general(
            incoming_ref[s], held_ref[...], (((1,), (1,)), ((), ())), preferred_element_type=f32
        )
        products_ref[pl.ds(s * layers + layer, 1), :] = jnp.sum(jnp.where(same, every, 0.0), axis=0, keepdims=True)


def generate_kernel(
    parts_ref, weight_ref, scaled_ref,
    mixing_ref, slope_ref, preact_ref, factor_ref, payload_ref,
):
    hidden = weight_ref.shape[0]
    parts = parts_ref[...].astype(f32)
    packed = (parts[0] + parts[1]) + (parts[2] + parts[3])
    factor = lax.rsqrt(packed[:, hidden : hidden + 1] / D + epsilon)
    preact = factor * packed[:, :hidden]
    factor_ref[...] = jnp.broadcast_to(factor, factor_ref.shape)
    preact_ref[...] = preact
    inside = 0.7978845608028654 * (preact + 0.044715 * (preact * preact * preact))
    bent = jnp.tanh(inside)
    active = (0.5 * preact * (1.0 + bent)).astype(bf16)
    slope = 0.5 * (1.0 + bent) + 0.5 * preact * (1.0 - bent * bent) * (
        0.7978845608028654 * (1.0 + 3 * 0.044715 * (preact * preact))
    )
    slope_ref[...] = slope
    first = (slope * factor).T.astype(bf16)
    second = active.astype(f32).T.astype(bf16)
    members, chunk = payload_ref.shape[0], payload_ref.shape[1] - 2 * hidden
    for m in range(members):
        payload_ref[m, :chunk] = scaled_ref[m * chunk : (m + 1) * chunk]
        payload_ref[m, chunk : chunk + hidden] = first
        payload_ref[m, chunk + hidden :] = second
    mixing_ref[...] = jnp.dot(active, weight_ref[...], preferred_element_type=f32)


def own_kernel(layers, place_ref, held_ref, incoming_ref, products_ref):
    products_ref[...] = jnp.zeros_like(products_ref)
    put_products(held_ref, incoming_ref, products_ref, place_ref[0], layers)


def depth_kernel(turn, layers, place_ref, even_ref, odd_ref, incoming_ref, before_ref, products_ref):
    products_ref[...] = before_ref[...]
    layer = (place_ref[0] - (turn - 1)) & (layers - 1)
    for chain, held_ref in enumerate((even_ref, odd_ref)):

        @pl.when(place_ref[1] == chain)
        def _():
            put_products(held_ref, incoming_ref, products_ref, layer, layers)


def tiles(shape):
    return [(slice(r, r + 16), slice(at, at + LANES)) for r in range(0, shape[0], 16) for at in range(0, shape[1], LANES)]


def hop_kernel(turn, chain, layers, place_ref, held_ref, incoming_ref, mixing_ref, sent_ref):
    rising = place_ref[1] == chain

    @pl.when(rising)
    def _():
        sent_ref[...] = held_ref[...]

    @pl.when(jnp.logical_not(rising))
    def _():
        weights = weights_of(mixing_ref[...], place_ref[0] + turn - LAG - layers, layers)
        for rows, lanes in tiles(sent_ref.shape):
            total = add_term(rows, lanes, weights, incoming_ref, held_ref[rows, lanes].astype(f32))
            sent_ref[rows, lanes] = total.astype(bf16)


def finish_kernel(layers, place_ref, even_ref, odd_ref, incoming_ref, mixing_ref, generated_ref, out_ref):
    even = place_ref[1] == 0
    weights = weights_of(mixing_ref[...], place_ref[0], layers)
    for rows, lanes in tiles(out_ref.shape):
        came = jnp.where(even, odd_ref[rows, lanes].astype(f32), even_ref[rows, lanes].astype(f32))
        total = add_term(rows, lanes, weights, incoming_ref, came)
        out_ref[rows, lanes] = (total + generated_ref[rows, lanes]).astype(bf16)


def depth_grad_kernel(parts_ref, spread_ref):
    parts = parts_ref[...]
    turned = ((parts[0] + parts[1]) + (parts[2] + parts[3])).astype(bf16)
    for m in range(spread_ref.shape[0]):
        spread_ref[m] = turned


def chunk_kernel(depth_ref, weight_ref, gathered_ref, mine_ref):
    hidden = weight_ref.shape[0]
    members, rows = gathered_ref.shape[0], gathered_ref.shape[1] - 2 * hidden
    first = jnp.zeros((rows, hidden), f32)
    second = jnp.zeros((depth_ref.shape[1], hidden), f32)
    across = (((1,), (1,)), ((), ()))
    for m in range(members):
        depth = depth_ref[m]
        dactive = jnp.dot(weight_ref[...], depth, preferred_element_type=f32)
        scaled_grad = (dactive * gathered_ref[m, rows : rows + hidden].astype(f32)).astype(bf16)
        first = first + lax.dot_general(gathered_ref[m, :rows], scaled_grad, across, preferred_element_type=f32)
        second = second + lax.dot_general(depth, gathered_ref[m, rows + hidden :], across, preferred_element_type=f32)
    mine_ref[:rows] = first.astype(bf16)
    mine_ref[rows:] = second.astype(bf16)


def gradient_kernel(depth_ref, weight_ref, slope_ref, preact_ref, factor_ref, scaled_grad_ref, back_ref):
    depth_grads = depth_ref[0].astype(f32).T.astype(bf16)
    dactive = jnp.dot(depth_grads, weight_ref[...], preferred_element_type=f32)
    dpreact = dactive * slope_ref[...]
    factor = factor_ref[...][:, :1]
    inner = jnp.sum(dpreact * preact_ref[...], axis=1, keepdims=True)
    back_ref[...] = jnp.broadcast_to(factor * factor * inner / D, back_ref.shape)
    scaled_grad_ref[...] = (dpreact * factor).astype(bf16)


def on_device(outputs, cotangents, gains, first_weight, second_weight):
    layers = lax.axis_size("pipe")
    section = lax.axis_index("pipe")
    size = lax.axis_size("dp")
    last = layers - 1
    current = outputs[0]
    incoming = cotangents[:, 0]
    tokens, width = current.shape
    hidden = first_weight.shape[2]
    columns = 4 * layers
    shape = jax.ShapeDtypeStruct
    place = jnp.stack([section, lax.axis_index("dp") & 1]).astype(jnp.int32)

    def hop(array, turn, chain):
        pairs = [(k * size + i, (k + 1) * size + i) for k in range(turn - 1, last) for i in range(chain, size, 2)]
        if turn > LAG:
            pairs += [
                (k * size + i, (k - 1) * size + i) for k in range(layers + LAG - turn, layers) for i in range(1 - chain, size, 2)
            ]
        return lax.ppermute(array, ("pipe", "dp"), pairs)

    groups = [[x * 4 + z * 2 + core for x in range(size // 4) for core in range(2)] for z in range(2)]
    members = size // 2
    index = lax.axis_index("dp")
    chunk = width // members

    packed, scaled_turned = call(
        project_kernel,
        [shape((4, tokens, hidden + 128), bf16), shape((width, tokens), bf16)],
        2 * tokens * width * hidden,
        4 * width * (tokens + hidden),
        count=3,
    )(current, gains, first_weight[0])
    packed = lax.all_to_all(packed, "tensor", 0, 0, tiled=True)
    chains = [hop(current, 1, chain) for chain in range(2)]
    packed, *chains = lax.optimization_barrier((packed, *chains))
    mixing, slope, preact, factor, payload = call(
        generate_kernel,
        [
            shape((tokens, columns), f32),
            shape((tokens, hidden), f32),
            shape((tokens, hidden), f32),
            shape((tokens, 128), f32),
            shape((members, chunk + 2 * hidden, tokens), bf16),
        ],
        2 * tokens * hidden * columns,
        20 * tokens * hidden,
        count=3,
    )(packed, second_weight[0], scaled_turned)
    [products] = call(
        functools.partial(own_kernel, layers),
        [shape((columns, tokens), f32)],
        8 * tokens * width,
        10 * tokens * width,
        smem=1,
        count=3,
    )(place, current, incoming)

    def advance(turn, chain):
        if turn <= LAG:
            return hop(chains[chain], turn, chain)
        [sent] = call(
            functools.partial(hop_kernel, turn, chain, layers),
            [shape((tokens, width), bf16)],
            8 * tokens * width,
            12 * tokens * width,
            smem=1,
            count=4,
        )(place, chains[chain], incoming, mixing)
        return hop(sent, turn, chain)

    for turn in range(2, layers + 1):
        held = chains
        chains = [advance(turn, chain) for chain in range(2)]
        [products] = call(
            functools.partial(depth_kernel, turn, layers),
            [shape((columns, tokens), f32)],
            8 * tokens * width,
            10 * tokens * width,
            smem=1,
            count=5,
        )(place, *held, incoming, products)
        if turn == LAG + 1:
            payload, products = lax.optimization_barrier((payload, products))
            gathered = lax.all_to_all(payload, "dp", 0, 0, axis_index_groups=groups, tiled=True)
        if turn == 2 * LAG + 1:
            gathered, products = lax.optimization_barrier((gathered, products))
        mixing, products = lax.optimization_barrier((mixing, products))

    spread = lax.all_to_all(jnp.broadcast_to(products[None], (4, columns, tokens)), "tensor", 0, 0, tiled=True)
    [depth_grads] = call(depth_grad_kernel, [shape((members, columns, tokens), bf16)], 0, 8 * columns * tokens, count=1)(spread)
    depth_all = lax.all_to_all(depth_grads, "dp", 0, 0, axis_index_groups=groups, tiled=True)
    [mine] = call(
        chunk_kernel,
        [shape((chunk + columns, hidden), bf16)],
        2 * tokens * width * hidden,
        4 * members * tokens * hidden,
        count=3,
    )(depth_all, second_weight[0], gathered)
    mine, *chains = lax.optimization_barrier((mine, *chains))
    other = lax.ppermute(mine, "dp", [(i, i ^ 2) for i in range(size)])
    total = mine.astype(f32) + other.astype(f32)
    divisor = tokens * size
    second_grads = total[chunk:].T / divisor
    spread = jnp.broadcast_to(total[None, :chunk].astype(bf16), (size // 4, chunk, hidden))
    along = [[x * 4 + rest for x in range(size // 4)] for rest in range(4)]
    for turn in range(layers + 1, layers + LAG):
        chains = [advance(turn, chain) for chain in range(2)]
    own = lax.all_to_all(spread, "dp", 0, 0, axis_index_groups=along, tiled=True)
    far = lax.ppermute(own, "dp", [(i, i ^ 1) for i in range(size)])
    scaled_grad, back = call(
        gradient_kernel,
        [shape((tokens, hidden), bf16), shape((tokens, 128), f32)],
        2 * tokens * hidden * columns,
        16 * tokens * hidden,
        count=5,
    )(depth_grads, second_weight[0].T, slope, preact, factor)

    weighted = lax.dot_general(scaled_grad, first_weight[0], (((1,), (1,)), ((), ())), preferred_element_type=f32)
    generated = weighted * gains[0].astype(f32)[None] - current.astype(f32) * back[:, :1]
    [output_grads] = call(
        functools.partial(finish_kernel, layers),
        [shape((tokens, width), bf16)],
        8 * tokens * width,
        16 * tokens * width,
        smem=1,
        count=6,
    )(place, chains[0], chains[1], incoming, mixing, generated)
    far, output_grads = lax.optimization_barrier((far, output_grads))
    near = (index & 1) == 0
    summed = jnp.stack([jnp.where(near, own, far), jnp.where(near, far, own)], axis=1)
    first_grads = summed.astype(f32).reshape(width, hidden) / divisor
    return (output_grads[None], first_grads[None], second_grads[None])


def solution(mesh):
    placed = (
        P("pipe", "dp", "tensor"),
        P(None, "pipe", "dp", "tensor"),
        P("pipe", "tensor"),
        P("pipe", "tensor", None),
        P("pipe", None, None),
    )
    return jax.shard_map(
        on_device,
        mesh=mesh,
        in_specs=placed,
        out_specs=(P("pipe", "dp", "tensor"), P("pipe", "tensor", None), P("pipe", None, None)),
        check_vma=False,
    )
```

```python
import functools

import jax
import jax.numpy as jnp
from jax import lax
from jax.experimental import pallas as pl
from jax.experimental.pallas import tpu as pltpu
from jax.sharding import PartitionSpec as P

D = 6144
epsilon = 1e-06
LAG = 3
LANES = 512

f32 = jnp.float32
bf16 = jnp.bfloat16


def call(kernel, shapes, flops, moved, scratch=(), smem=0, count=0):
    return pl.pallas_call(
        kernel,
        out_shape=shapes,
        in_specs=[pl.BlockSpec(memory_space=pltpu.SMEM)] * smem
        + [pl.BlockSpec(memory_space=pltpu.VMEM)] * (count - smem),
        out_specs=[pl.BlockSpec(memory_space=pltpu.VMEM)] * len(shapes),
        scratch_shapes=list(scratch),
        compiler_params=pltpu.CompilerParams(vmem_limit_bytes=20 * 1024 * 1024),
        cost_estimate=pl.CostEstimate(flops=flops, bytes_accessed=moved, transcendentals=0),
    )


def project_kernel(x_ref, gain_ref, weight_ref, packed_ref, turned_ref):
    hidden = weight_ref.shape[1]
    tokens = x_ref.shape[0]
    x = x_ref[...].astype(f32)
    scaled = (x * gain_ref[...].astype(f32)).astype(bf16)
    turned_ref[...] = scaled.astype(f32).T.astype(bf16)
    projected = jnp.dot(scaled, weight_ref[...], preferred_element_type=f32).astype(bf16)
    squares = jnp.broadcast_to(jnp.sum(x * x, axis=1, keepdims=True), (tokens, 128)).astype(bf16)
    for m in range(packed_ref.shape[0]):
        packed_ref[m, :, :hidden] = projected
        packed_ref[m, :, hidden:] = squares


def weights_of(mixed, layer, layers):
    lane = lax.broadcasted_iota(jnp.int32, mixed.shape, 1)
    return [
        jnp.sum(jnp.where(lane == jnp.where(layer < 0, -1, s * layers + layer), mixed, 0.0), axis=1, keepdims=True)
        for s in range(4)
    ]


def add_term(rows, lanes, weights, incoming_ref, total):
    for s in range(4):
        total = total + weights[s][rows] * incoming_ref[s, rows, lanes].astype(f32)
    return total


def put_products(held_ref, incoming_ref, products_ref, layer, layers):
    tokens = held_ref.shape[0]
    same = lax.broadcasted_iota(jnp.int32, (tokens, tokens), 0) == lax.broadcasted_iota(jnp.int32, (tokens, tokens), 1)
    for s in range(4):
        every = lax.dot_general(
            incoming_ref[s], held_ref[...], (((1,), (1,)), ((), ())), preferred_element_type=f32
        )
        products_ref[pl.ds(s * layers + layer, 1), :] = jnp.sum(jnp.where(same, every, 0.0), axis=0, keepdims=True)


def generate_kernel(
    parts_ref, weight_ref, scaled_ref,
    mixing_ref, slope_ref, preact_ref, factor_ref, payload_ref,
):
    hidden = weight_ref.shape[0]
    parts = parts_ref[...].astype(f32)
    packed = (parts[0] + parts[1]) + (parts[2] + parts[3])
    factor = lax.rsqrt(packed[:, hidden : hidden + 1] / D + epsilon)
    preact = factor * packed[:, :hidden]
    factor_ref[...] = jnp.broadcast_to(factor, factor_ref.shape)
    preact_ref[...] = preact
    inside = 0.7978845608028654 * (preact + 0.044715 * (preact * preact * preact))
    bent = jnp.tanh(inside)
    active = (0.5 * preact * (1.0 + bent)).astype(bf16)
    slope = 0.5 * (1.0 + bent) + 0.5 * preact * (1.0 - bent * bent) * (
        0.7978845608028654 * (1.0 + 3 * 0.044715 * (preact * preact))
    )
    slope_ref[...] = slope
    first = (slope * factor).T.astype(bf16)
    second = active.astype(f32).T.astype(bf16)
    members, chunk = payload_ref.shape[0], payload_ref.shape[1] - 2 * hidden
    for m in range(members):
        payload_ref[m, :chunk] = scaled_ref[m * chunk : (m + 1) * chunk]
        payload_ref[m, chunk : chunk + hidden] = first
        payload_ref[m, chunk + hidden :] = second
    mixing_ref[...] = jnp.dot(active, weight_ref[...], preferred_element_type=f32)


def own_kernel(layers, place_ref, held_ref, incoming_ref, products_ref):
    products_ref[...] = jnp.zeros_like(products_ref)
    put_products(held_ref, incoming_ref, products_ref, place_ref[0], layers)


def depth_kernel(turn, layers, place_ref, even_ref, odd_ref, incoming_ref, before_ref, products_ref):
    products_ref[...] = before_ref[...]
    layer = (place_ref[0] - (turn - 1)) & (layers - 1)
    for chain, held_ref in enumerate((even_ref, odd_ref)):

        @pl.when(place_ref[1] == chain)
        def _():
            put_products(held_ref, incoming_ref, products_ref, layer, layers)


def tiles(shape):
    return [(slice(r, r + 16), slice(at, at + LANES)) for r in range(0, shape[0], 16) for at in range(0, shape[1], LANES)]


def hop_kernel(turn, chain, layers, place_ref, held_ref, incoming_ref, mixing_ref, sent_ref):
    rising = place_ref[1] == chain

    @pl.when(rising)
    def _():
        sent_ref[...] = held_ref[...]

    @pl.when(jnp.logical_not(rising))
    def _():
        weights = weights_of(mixing_ref[...], place_ref[0] + turn - LAG - layers, layers)
        for rows, lanes in tiles(sent_ref.shape):
            total = add_term(rows, lanes, weights, incoming_ref, held_ref[rows, lanes].astype(f32))
            sent_ref[rows, lanes] = total.astype(bf16)


def finish_kernel(layers, place_ref, even_ref, odd_ref, incoming_ref, mixing_ref, generated_ref, out_ref):
    even = place_ref[1] == 0
    weights = weights_of(mixing_ref[...], place_ref[0], layers)
    for rows, lanes in tiles(out_ref.shape):
        came = jnp.where(even, odd_ref[rows, lanes].astype(f32), even_ref[rows, lanes].astype(f32))
        total = add_term(rows, lanes, weights, incoming_ref, came)
        out_ref[rows, lanes] = (total + generated_ref[rows, lanes]).astype(bf16)


def depth_grad_kernel(parts_ref, spread_ref):
    parts = parts_ref[...]
    turned = ((parts[0] + parts[1]) + (parts[2] + parts[3])).astype(bf16)
    for m in range(spread_ref.shape[0]):
        spread_ref[m] = turned


def chunk_kernel(depth_ref, weight_ref, gathered_ref, mine_ref):
    hidden = weight_ref.shape[0]
    members, rows = gathered_ref.shape[0], gathered_ref.shape[1] - 2 * hidden
    first = jnp.zeros((rows, hidden), f32)
    second = jnp.zeros((depth_ref.shape[1], hidden), f32)
    across = (((1,), (1,)), ((), ()))
    for m in range(members):
        depth = depth_ref[m]
        dactive = jnp.dot(weight_ref[...], depth, preferred_element_type=f32)
        scaled_grad = (dactive * gathered_ref[m, rows : rows + hidden].astype(f32)).astype(bf16)
        first = first + lax.dot_general(gathered_ref[m, :rows], scaled_grad, across, preferred_element_type=f32)
        second = second + lax.dot_general(depth, gathered_ref[m, rows + hidden :], across, preferred_element_type=f32)
    mine_ref[:rows] = first.astype(bf16)
    mine_ref[rows:] = second.astype(bf16)


def gradient_kernel(depth_ref, weight_ref, slope_ref, preact_ref, factor_ref, scaled_grad_ref, back_ref):
    depth_grads = depth_ref[0].astype(f32).T.astype(bf16)
    dactive = jnp.dot(depth_grads, weight_ref[...], preferred_element_type=f32)
    dpreact = dactive * slope_ref[...]
    factor = factor_ref[...][:, :1]
    inner = jnp.sum(dpreact * preact_ref[...], axis=1, keepdims=True)
    back_ref[...] = jnp.broadcast_to(factor * factor * inner / D, back_ref.shape)
    scaled_grad_ref[...] = (dpreact * factor).astype(bf16)


def on_device(outputs, cotangents, gains, first_weight, second_weight):
    layers = lax.axis_size("pipe")
    section = lax.axis_index("pipe")
    size = lax.axis_size("dp")
    last = layers - 1
    current = outputs[0]
    incoming = cotangents[:, 0]
    tokens, width = current.shape
    hidden = first_weight.shape[2]
    columns = 4 * layers
    shape = jax.ShapeDtypeStruct
    place = jnp.stack([section, lax.axis_index("dp") & 1]).astype(jnp.int32)

    def hop(array, turn, chain):
        pairs = [(k * size + i, (k + 1) * size + i) for k in range(turn - 1, last) for i in range(chain, size, 2)]
        if turn > LAG:
            pairs += [
                (k * size + i, (k - 1) * size + i) for k in range(layers + LAG - turn, layers) for i in range(1 - chain, size, 2)
            ]
        return lax.ppermute(array, ("pipe", "dp"), pairs)

    groups = [[x * 4 + z * 2 + core for x in range(size // 4) for core in range(2)] for z in range(2)]
    members = size // 2
    index = lax.axis_index("dp")
    chunk = width // members

    packed, scaled_turned = call(
        project_kernel,
        [shape((4, tokens, hidden + 128), bf16), shape((width, tokens), bf16)],
        2 * tokens * width * hidden,
        4 * width * (tokens + hidden),
        count=3,
    )(current, gains, first_weight[0])
    packed = lax.all_to_all(packed, "tensor", 0, 0, tiled=True)
    chains = [hop(current, 1, chain) for chain in range(2)]
    packed, *chains = lax.optimization_barrier((packed, *chains))
    mixing, slope, preact, factor, payload = call(
        generate_kernel,
        [
            shape((tokens, columns), f32),
            shape((tokens, hidden), f32),
            shape((tokens, hidden), f32),
            shape((tokens, 128), f32),
            shape((members, chunk + 2 * hidden, tokens), bf16),
        ],
        2 * tokens * hidden * columns,
        20 * tokens * hidden,
        count=3,
    )(packed, second_weight[0], scaled_turned)
    [products] = call(
        functools.partial(own_kernel, layers),
        [shape((columns, tokens), f32)],
        8 * tokens * width,
        10 * tokens * width,
        smem=1,
        count=3,
    )(place, current, incoming)

    def advance(turn, chain):
        if turn <= LAG:
            return hop(chains[chain], turn, chain)
        [sent] = call(
            functools.partial(hop_kernel, turn, chain, layers),
            [shape((tokens, width), bf16)],
            8 * tokens * width,
            12 * tokens * width,
            smem=1,
            count=4,
        )(place, chains[chain], incoming, mixing)
        return hop(sent, turn, chain)

    for turn in range(2, layers + 1):
        held = chains
        chains = [advance(turn, chain) for chain in range(2)]
        [products] = call(
            functools.partial(depth_kernel, turn, layers),
            [shape((columns, tokens), f32)],
            8 * tokens * width,
            10 * tokens * width,
            smem=1,
            count=5,
        )(place, *held, incoming, products)
        if turn == 2:
            payload, products = lax.optimization_barrier((payload, products))
            gathered = lax.all_to_all(payload, "dp", 0, 0, axis_index_groups=groups, tiled=True)
        if turn == LAG + 2:
            gathered, products = lax.optimization_barrier((gathered, products))
        mixing, products = lax.optimization_barrier((mixing, products))

    spread = lax.all_to_all(jnp.broadcast_to(products[None], (4, columns, tokens)), "tensor", 0, 0, tiled=True)
    [depth_grads] = call(depth_grad_kernel, [shape((members, columns, tokens), bf16)], 0, 8 * columns * tokens, count=1)(spread)
    depth_all = lax.all_to_all(depth_grads, "dp", 0, 0, axis_index_groups=groups, tiled=True)
    [mine] = call(
        chunk_kernel,
        [shape((chunk + columns, hidden), bf16)],
        2 * tokens * width * hidden,
        4 * members * tokens * hidden,
        count=3,
    )(depth_all, second_weight[0], gathered)
    mine, *chains = lax.optimization_barrier((mine, *chains))
    other = lax.ppermute(mine, "dp", [(i, i ^ 2) for i in range(size)])
    total = mine.astype(f32) + other.astype(f32)
    divisor = tokens * size
    second_grads = total[chunk:].T / divisor
    spread = jnp.broadcast_to(total[None, :chunk].astype(bf16), (size // 4, chunk, hidden))
    along = [[x * 4 + rest for x in range(size // 4)] for rest in range(4)]
    own = lax.all_to_all(spread, "dp", 0, 0, axis_index_groups=along, tiled=True)
    for turn in range(layers + 1, layers + LAG):
        chains = [advance(turn, chain) for chain in range(2)]
        if turn == layers + 1:
            own, *chains = lax.optimization_barrier((own, *chains))
    far = lax.ppermute(own, "dp", [(i, i ^ 1) for i in range(size)])
    near = (index & 1) == 0
    summed = jnp.stack([jnp.where(near, own, far), jnp.where(near, far, own)], axis=1)
    first_grads = summed.astype(f32).reshape(width, hidden) / divisor

    scaled_grad, back = call(
        gradient_kernel,
        [shape((tokens, hidden), bf16), shape((tokens, 128), f32)],
        2 * tokens * hidden * columns,
        16 * tokens * hidden,
        count=5,
    )(depth_grads, second_weight[0].T, slope, preact, factor)

    weighted = lax.dot_general(scaled_grad, first_weight[0], (((1,), (1,)), ((), ())), preferred_element_type=f32)
    generated = weighted * gains[0].astype(f32)[None] - current.astype(f32) * back[:, :1]
    [output_grads] = call(
        functools.partial(finish_kernel, layers),
        [shape((tokens, width), bf16)],
        8 * tokens * width,
        16 * tokens * width,
        smem=1,
        count=6,
    )(place, chains[0], chains[1], incoming, mixing, generated)
    return (output_grads[None], first_grads[None], second_grads[None])


def solution(mesh):
    placed = (
        P("pipe", "dp", "tensor"),
        P(None, "pipe", "dp", "tensor"),
        P("pipe", "tensor"),
        P("pipe", "tensor", None),
        P("pipe", None, None),
    )
    return jax.shard_map(
        on_device,
        mesh=mesh,
        in_specs=placed,
        out_specs=(P("pipe", "dp", "tensor"), P("pipe", "tensor", None), P("pipe", None, None)),
        check_vma=False,
    )
```

```python
import functools

import jax
import jax.numpy as jnp
from jax import lax
from jax.experimental import pallas as pl
from jax.experimental.pallas import tpu as pltpu
from jax.sharding import PartitionSpec as P

D = 6144
epsilon = 1e-06
LAG = 3
LANES = 512

f32 = jnp.float32
bf16 = jnp.bfloat16


def call(kernel, shapes, flops, moved, scratch=(), smem=0, count=0):
    return pl.pallas_call(
        kernel,
        out_shape=shapes,
        in_specs=[pl.BlockSpec(memory_space=pltpu.SMEM)] * smem
        + [pl.BlockSpec(memory_space=pltpu.VMEM)] * (count - smem),
        out_specs=[pl.BlockSpec(memory_space=pltpu.VMEM)] * len(shapes),
        scratch_shapes=list(scratch),
        compiler_params=pltpu.CompilerParams(vmem_limit_bytes=20 * 1024 * 1024),
        cost_estimate=pl.CostEstimate(flops=flops, bytes_accessed=moved, transcendentals=0),
    )


def project_kernel(x_ref, gain_ref, weight_ref, packed_ref, turned_ref):
    hidden = weight_ref.shape[1]
    tokens = x_ref.shape[0]
    x = x_ref[...].astype(f32)
    scaled = (x * gain_ref[...].astype(f32)).astype(bf16)
    turned_ref[...] = scaled.astype(f32).T.astype(bf16)
    projected = jnp.dot(scaled, weight_ref[...], preferred_element_type=f32).astype(bf16)
    squares = jnp.broadcast_to(jnp.sum(x * x, axis=1, keepdims=True), (tokens, 128)).astype(bf16)
    for m in range(packed_ref.shape[0]):
        packed_ref[m, :, :hidden] = projected
        packed_ref[m, :, hidden:] = squares


def weights_of(mixed, layer, layers):
    lane = lax.broadcasted_iota(jnp.int32, mixed.shape, 1)
    return [
        jnp.sum(jnp.where(lane == jnp.where(layer < 0, -1, s * layers + layer), mixed, 0.0), axis=1, keepdims=True)
        for s in range(4)
    ]


def add_term(rows, lanes, weights, incoming_ref, total):
    for s in range(4):
        total = total + weights[s][rows] * incoming_ref[s, rows, lanes].astype(f32)
    return total


def put_products(held_ref, incoming_ref, products_ref, layer, layers):
    tokens = held_ref.shape[0]
    same = lax.broadcasted_iota(jnp.int32, (tokens, tokens), 0) == lax.broadcasted_iota(jnp.int32, (tokens, tokens), 1)
    for s in range(4):
        every = lax.dot_general(
            incoming_ref[s], held_ref[...], (((1,), (1,)), ((), ())), preferred_element_type=f32
        )
        products_ref[pl.ds(s * layers + layer, 1), :] = jnp.sum(jnp.where(same, every, 0.0), axis=0, keepdims=True)


def generate_kernel(
    parts_ref, weight_ref, scaled_ref,
    mixing_ref, slope_ref, preact_ref, factor_ref, payload_ref,
):
    hidden = weight_ref.shape[0]
    parts = parts_ref[...].astype(f32)
    packed = (parts[0] + parts[1]) + (parts[2] + parts[3])
    factor = lax.rsqrt(packed[:, hidden : hidden + 1] / D + epsilon)
    preact = factor * packed[:, :hidden]
    factor_ref[...] = jnp.broadcast_to(factor, factor_ref.shape)
    preact_ref[...] = preact
    inside = 0.7978845608028654 * (preact + 0.044715 * (preact * preact * preact))
    bent = jnp.tanh(inside)
    active = (0.5 * preact * (1.0 + bent)).astype(bf16)
    slope = 0.5 * (1.0 + bent) + 0.5 * preact * (1.0 - bent * bent) * (
        0.7978845608028654 * (1.0 + 3 * 0.044715 * (preact * preact))
    )
    slope_ref[...] = slope
    first = (slope * factor).T.astype(bf16)
    second = active.astype(f32).T.astype(bf16)
    members, chunk = payload_ref.shape[0], payload_ref.shape[1] - 2 * hidden
    for m in range(members):
        payload_ref[m, :chunk] = scaled_ref[m * chunk : (m + 1) * chunk]
        payload_ref[m, chunk : chunk + hidden] = first
        payload_ref[m, chunk + hidden :] = second
    mixing_ref[...] = jnp.dot(active, weight_ref[...], preferred_element_type=f32)


def own_kernel(layers, place_ref, held_ref, incoming_ref, products_ref):
    products_ref[...] = jnp.zeros_like(products_ref)
    put_products(held_ref, incoming_ref, products_ref, place_ref[0], layers)


def depth_kernel(turn, layers, place_ref, even_ref, odd_ref, incoming_ref, before_ref, products_ref):
    products_ref[...] = before_ref[...]
    layer = (place_ref[0] - (turn - 1)) & (layers - 1)
    for chain, held_ref in enumerate((even_ref, odd_ref)):

        @pl.when(place_ref[1] == chain)
        def _():
            put_products(held_ref, incoming_ref, products_ref, layer, layers)


def tiles(shape):
    return [(slice(r, r + 16), slice(at, at + LANES)) for r in range(0, shape[0], 16) for at in range(0, shape[1], LANES)]


def hop_kernel(turn, chain, layers, place_ref, held_ref, incoming_ref, mixing_ref, sent_ref):
    rising = place_ref[1] == chain

    @pl.when(rising)
    def _():
        sent_ref[...] = held_ref[...]

    @pl.when(jnp.logical_not(rising))
    def _():
        weights = weights_of(mixing_ref[...], place_ref[0] + turn - LAG - layers, layers)
        for rows, lanes in tiles(sent_ref.shape):
            total = add_term(rows, lanes, weights, incoming_ref, held_ref[rows, lanes].astype(f32))
            sent_ref[rows, lanes] = total.astype(bf16)


def finish_kernel(layers, place_ref, even_ref, odd_ref, incoming_ref, mixing_ref, generated_ref, out_ref):
    even = place_ref[1] == 0
    weights = weights_of(mixing_ref[...], place_ref[0], layers)
    for rows, lanes in tiles(out_ref.shape):
        came = jnp.where(even, odd_ref[rows, lanes].astype(f32), even_ref[rows, lanes].astype(f32))
        total = add_term(rows, lanes, weights, incoming_ref, came)
        out_ref[rows, lanes] = (total + generated_ref[rows, lanes]).astype(bf16)


def depth_grad_kernel(parts_ref, spread_ref):
    parts = parts_ref[...]
    turned = ((parts[0] + parts[1]) + (parts[2] + parts[3])).astype(bf16)
    for m in range(spread_ref.shape[0]):
        spread_ref[m] = turned


def chunk_kernel(depth_ref, weight_ref, gathered_ref, mine_ref):
    hidden = weight_ref.shape[0]
    members, rows = gathered_ref.shape[0], gathered_ref.shape[1] - 2 * hidden
    first = jnp.zeros((rows, hidden), f32)
    second = jnp.zeros((depth_ref.shape[1], hidden), f32)
    across = (((1,), (1,)), ((), ()))
    for m in range(members):
        depth = depth_ref[m]
        dactive = jnp.dot(weight_ref[...], depth, preferred_element_type=f32)
        scaled_grad = (dactive * gathered_ref[m, rows : rows + hidden].astype(f32)).astype(bf16)
        first = first + lax.dot_general(gathered_ref[m, :rows], scaled_grad, across, preferred_element_type=f32)
        second = second + lax.dot_general(depth, gathered_ref[m, rows + hidden :], across, preferred_element_type=f32)
    mine_ref[:rows] = first.astype(bf16)
    mine_ref[rows:] = second.astype(bf16)


def gradient_kernel(depth_ref, weight_ref, slope_ref, preact_ref, factor_ref, scaled_grad_ref, back_ref):
    depth_grads = depth_ref[0].astype(f32).T.astype(bf16)
    dactive = jnp.dot(depth_grads, weight_ref[...], preferred_element_type=f32)
    dpreact = dactive * slope_ref[...]
    factor = factor_ref[...][:, :1]
    inner = jnp.sum(dpreact * preact_ref[...], axis=1, keepdims=True)
    back_ref[...] = jnp.broadcast_to(factor * factor * inner / D, back_ref.shape)
    scaled_grad_ref[...] = (dpreact * factor).astype(bf16)


def on_device(outputs, cotangents, gains, first_weight, second_weight):
    layers = lax.axis_size("pipe")
    section = lax.axis_index("pipe")
    size = lax.axis_size("dp")
    last = layers - 1
    current = outputs[0]
    incoming = cotangents[:, 0]
    tokens, width = current.shape
    hidden = first_weight.shape[2]
    columns = 4 * layers
    shape = jax.ShapeDtypeStruct
    place = jnp.stack([section, lax.axis_index("dp") & 1]).astype(jnp.int32)

    def hop(array, turn, chain):
        pairs = [(k * size + i, (k + 1) * size + i) for k in range(turn - 1, last) for i in range(chain, size, 2)]
        if turn > LAG:
            pairs += [
                (k * size + i, (k - 1) * size + i) for k in range(layers + LAG - turn, layers) for i in range(1 - chain, size, 2)
            ]
        return lax.ppermute(array, ("pipe", "dp"), pairs)

    groups = [[x * 4 + z * 2 + core for x in range(size // 4) for core in range(2)] for z in range(2)]
    members = size // 2
    index = lax.axis_index("dp")
    chunk = width // members

    packed, scaled_turned = call(
        project_kernel,
        [shape((4, tokens, hidden + 128), bf16), shape((width, tokens), bf16)],
        2 * tokens * width * hidden,
        4 * width * (tokens + hidden),
        count=3,
    )(current, gains, first_weight[0])
    packed = lax.all_to_all(packed, "tensor", 0, 0, tiled=True)
    chains = [hop(current, 1, chain) for chain in range(2)]
    packed, *chains = lax.optimization_barrier((packed, *chains))
    mixing, slope, preact, factor, payload = call(
        generate_kernel,
        [
            shape((tokens, columns), f32),
            shape((tokens, hidden), f32),
            shape((tokens, hidden), f32),
            shape((tokens, 128), f32),
            shape((members, chunk + 2 * hidden, tokens), bf16),
        ],
        2 * tokens * hidden * columns,
        20 * tokens * hidden,
        count=3,
    )(packed, second_weight[0], scaled_turned)
    [products] = call(
        functools.partial(own_kernel, layers),
        [shape((columns, tokens), f32)],
        8 * tokens * width,
        10 * tokens * width,
        smem=1,
        count=3,
    )(place, current, incoming)

    def advance(turn, chain):
        if turn <= LAG:
            return hop(chains[chain], turn, chain)
        [sent] = call(
            functools.partial(hop_kernel, turn, chain, layers),
            [shape((tokens, width), bf16)],
            8 * tokens * width,
            12 * tokens * width,
            smem=1,
            count=4,
        )(place, chains[chain], incoming, mixing)
        return hop(sent, turn, chain)

    for turn in range(2, layers + 1):
        held = chains
        chains = [advance(turn, chain) for chain in range(2)]
        [products] = call(
            functools.partial(depth_kernel, turn, layers),
            [shape((columns, tokens), f32)],
            8 * tokens * width,
            10 * tokens * width,
            smem=1,
            count=5,
        )(place, *held, incoming, products)
        if turn == 2:
            payload, products = lax.optimization_barrier((payload, products))
            gathered = lax.all_to_all(payload, "dp", 0, 0, axis_index_groups=groups, tiled=True)
        if turn == LAG + 2:
            gathered, products = lax.optimization_barrier((gathered, products))
        mixing, products = lax.optimization_barrier((mixing, products))

    spread = lax.all_to_all(jnp.broadcast_to(products[None], (4, columns, tokens)), "tensor", 0, 0, tiled=True)
    [depth_grads] = call(depth_grad_kernel, [shape((members, columns, tokens), bf16)], 0, 8 * columns * tokens, count=1)(spread)
    depth_all = lax.all_to_all(depth_grads, "dp", 0, 0, axis_index_groups=groups, tiled=True)
    [mine] = call(
        chunk_kernel,
        [shape((chunk + columns, hidden), bf16)],
        2 * tokens * width * hidden,
        4 * members * tokens * hidden,
        count=3,
    )(depth_all, second_weight[0], gathered)
    mine, *chains = lax.optimization_barrier((mine, *chains))
    other = lax.ppermute(mine, "dp", [(i, i ^ 2) for i in range(size)])
    total = mine.astype(f32) + other.astype(f32)
    divisor = tokens * size
    second_grads = total[chunk:].T / divisor
    spread = jnp.broadcast_to(total[None, :chunk].astype(bf16), (size // 4, chunk, hidden))
    along = [[x * 4 + rest for x in range(size // 4)] for rest in range(4)]
    for turn in range(layers + 1, layers + LAG):
        chains = [advance(turn, chain) for chain in range(2)]
    own = lax.all_to_all(spread, "dp", 0, 0, axis_index_groups=along, tiled=True)
    own, *chains = lax.optimization_barrier((own, *chains))
    far = lax.ppermute(own, "dp", [(i, i ^ 1) for i in range(size)])
    near = (index & 1) == 0
    summed = jnp.stack([jnp.where(near, own, far), jnp.where(near, far, own)], axis=1)
    first_grads = summed.astype(f32).reshape(width, hidden) / divisor

    scaled_grad, back = call(
        gradient_kernel,
        [shape((tokens, hidden), bf16), shape((tokens, 128), f32)],
        2 * tokens * hidden * columns,
        16 * tokens * hidden,
        count=5,
    )(depth_grads, second_weight[0].T, slope, preact, factor)

    weighted = lax.dot_general(scaled_grad, first_weight[0], (((1,), (1,)), ((), ())), preferred_element_type=f32)
    generated = weighted * gains[0].astype(f32)[None] - current.astype(f32) * back[:, :1]
    [output_grads] = call(
        functools.partial(finish_kernel, layers),
        [shape((tokens, width), bf16)],
        8 * tokens * width,
        16 * tokens * width,
        smem=1,
        count=6,
    )(place, chains[0], chains[1], incoming, mixing, generated)
    return (output_grads[None], first_grads[None], second_grads[None])


def solution(mesh):
    placed = (
        P("pipe", "dp", "tensor"),
        P(None, "pipe", "dp", "tensor"),
        P("pipe", "tensor"),
        P("pipe", "tensor", None),
        P("pipe", None, None),
    )
    return jax.shard_map(
        on_device,
        mesh=mesh,
        in_specs=placed,
        out_specs=(P("pipe", "dp", "tensor"), P("pipe", "tensor", None), P("pipe", None, None)),
        check_vma=False,
    )
```
